256 devices in a mesh: seq: 4 (over x), half: 2 (over core), ctx: 32 (over y, z).
Axes of the slice: x: 4, y: 4, z: 8, core: 2. Of those that a mesh axis runs over, the one named last changes fastest.
Arguments:
- features: bfloat16 [12, 512, 32768], P('seq', None, ('half', 'ctx')), parts along dimension 0, may hold values from -6 to 6
- short_taps: float32 [7, 3, 512], replicated, may hold values from -2.5 to 2.5
- filters: float32 [512, 32768], P('ctx'), may hold values from -6 to 6
- skip: float32 [512], replicated, may hold values from -4 to 4
Outputs:
- mixed: bfloat16 [2048, 32768], P('seq', ('half', 'ctx')), parts along dimension 0
The draws below stay inside these ranges and needn't reach their ends.
There are 4 independent parts, one for each index of `seq`. The reference program is written for one: setup_inputs(seed, part) draws one part's arguments, and reference() takes and returns one part's arrays. A program takes and returns all parts, laid end to end along the dimension named above; an argument that names none is the same for every part. Nothing has to cross between parts.
All inputs are finite; a program needn't handle non-finite values.
Results may differ from the reference program's by a relative error of at most 0.005.
Values may be sent and summed in bfloat16 or wider, within the bound.
No kernel may reach another device: no remote copies, remote signals or barrier semaphores. Data moves between devices by JAX's collectives and lax.ppermute only.
A program may use at most 128 MiB of HBM per device.

```python
import math
import jax
import jax.numpy as jnp

TAPS = 7
CH = 512
L = 32768


def draw_filters(key, part):
    key_rate, key_noise, key_place = jax.random.split(key, 3)
    log_tau = jax.random.uniform(key_rate, (CH, 1), jnp.float32, math.log(30.0), math.log(4.0 * L))
    noise = jnp.clip(jax.random.normal(key_noise, (CH, L), jnp.float32), -6.0, 6.0)
    decay_len = jnp.exp(log_tau)
    position_slots = jax.random.randint(key_place, (CH, 3), 1, L)
    position_values = jnp.arange(L, dtype=jnp.float32)[None, :]
    decay_envelope = jnp.exp(-position_values / decay_len)
    for impulse_response in range(3):
        decay_envelope = decay_envelope * jnp.where(position_values >= position_slots[:, impulse_response:impulse_response + 1].astype(jnp.float32), 0.6, 1.0)
    ratio_gap = -jnp.expm1(-2.0 / decay_len)
    energy = (1.0 - jnp.exp(-2.0 * L / decay_len)) / ratio_gap
    return noise * decay_envelope * jax.lax.rsqrt(jnp.maximum(energy, 1.0))


def levels(stream_key, extent, pieces, low, top_value):
    gain, own = 1.0, jax.random.fold_in(stream_key, 6)
    for axis_at, parts in pieces:
        steps = jnp.exp(jax.random.uniform(jax.random.fold_in(own, axis_at), (parts,), jnp.float32, low / len(pieces), top_value / len(pieces)))
        gain = gain * jnp.repeat(steps, extent[axis_at] // parts).reshape([-1 if axis == axis_at else 1 for axis in range(len(extent))])
    return gain


def centred(rng, dims, spread, reach, cuts=(), kind=jnp.bfloat16):
    result = jax.random.normal(rng, dims, jnp.float32) * spread
    if len(cuts) > 0:
        result = levels(rng, dims, cuts, -0.22, 0.18) * result
    return jnp.clip(result, min=-reach, max=reach).astype(kind)


def setup_inputs(seed: int = 0, part: int = 0) -> dict:
    key_list = jax.random.split(jax.random.key(seed), 5)
    part_splits = jax.random.split(jax.random.fold_in(key_list[4], part), 5)
    return {
        "features": centred(part_splits[0], (3, CH, L), 1.0, 6.0, ((2, 64),)),
        "short_taps": centred(key_list[1], (TAPS, 3, CH), 0.4, 2.5, (), jnp.float32),
        "filters": draw_filters(jax.random.fold_in(key_list[4], 71), part),
        "skip": centred(key_list[3], (CH,), 1.0, 4.0, (), jnp.float32),
    }


def reference(features, short_taps, filters, skip):
    values = features.astype(jnp.float32)
    padded = jnp.pad(values, ((0, 0), (0, 0), (TAPS - 1, 0)))
    shaped = jnp.zeros_like(values)
    for offset in range(TAPS):
        start = TAPS - 1 - offset
        shaped = shaped + short_taps[offset][:, :, None] * padded[:, :, start:start + L]
    signal = shaped[1] * shaped[2]
    spec_signal = jnp.fft.rfft(signal, n=2 * L, axis=1)
    spec_filter = jnp.fft.rfft(filters, n=2 * L, axis=1)
    linear = jnp.fft.irfft(spec_signal * spec_filter, n=2 * L, axis=1)[:, :L]
    convolved = (linear + skip[:, None] * signal).astype(jnp.bfloat16)
    return (shaped[0] * convolved.astype(jnp.float32)).astype(jnp.bfloat16)
```

```python
import math

import jax
import jax.numpy as jnp
import ml_dtypes
import numpy as np
from jax import lax
from jax.experimental import pallas as pl
from jax.experimental.pallas import tpu as pltpu
from jax.sharding import PartitionSpec as P

TAPS = 7
EDGE = TAPS - 1
LANES = 128
N1 = 256
N2 = 128
TOTAL = N1 * N2
F32 = jnp.float32
BF16 = jnp.bfloat16


def halves(table):
    hi = table.astype(ml_dtypes.bfloat16)
    lo = (table - hi.astype(np.float64)).astype(ml_dtypes.bfloat16)
    return hi, lo


def transform_tables():
    k1 = np.arange(N1) + 0.25
    first = np.exp(-2j * np.pi * np.outer(k1, np.arange(N1)) / N1)
    twist = np.exp(-2j * np.pi * np.outer(k1, np.arange(N2)) / TOTAL)
    second = np.exp(-2j * np.pi * np.outer(np.arange(N2), np.arange(N2)) / N2)
    rows = np.concatenate([first.real, first.imag], 0)
    forward = np.block([[second.real, second.imag], [-second.imag, second.real]])
    backward = np.block([[second.real, -second.imag], [second.imag, second.real]])
    back_rows = np.concatenate([first.real.T, first.imag.T], 1)
    return dict(
        rows=halves(rows),
        twist=(twist.real.astype(np.float32), twist.imag.astype(np.float32)),
        forward=halves(forward),
        backward=halves(backward),
        back_rows=halves(back_rows),
    )


def mm(a, b):
    return jnp.dot(a, b, preferred_element_type=F32)


def split(x):
    hi = x.astype(BF16)
    return hi, (x - hi.astype(F32)).astype(BF16)


def mm3(x, whi, wlo):
    hi, lo = split(x)
    return mm(hi, whi) + mm(lo, whi) + mm(hi, wlo)


def twice(x):
    return jnp.concatenate([x, x], 1)


def tap_columns(taps_ref, branch, start, count):
    rows = [taps_ref[j, branch : branch + 1, pl.ds(start, count)] for j in range(TAPS)]
    rows.append(jnp.zeros((1, count), F32))
    return jnp.concatenate(rows, 0).T


GATE_ROWS = 128
STEP = 16


def gate_kernel(taps_ref, k_ref, v_ref, o_ref, ktap, vtap):
    start = pl.multiple_of(pl.program_id(0) * GATE_ROWS, GATE_ROWS)
    ktap[...] = tap_columns(taps_ref, 1, start, GATE_ROWS)
    vtap[...] = tap_columns(taps_ref, 2, start, GATE_ROWS)
    lane = lax.broadcasted_iota(jnp.int32, (STEP, LANES), 1)

    def step(g, carry):
        at = pl.ds(pl.multiple_of(g * STEP, STEP), STEP)
        k = k_ref[0, at, :].astype(F32)
        v = v_ref[0, at, :].astype(F32)
        kt, vt = ktap[at, :], vtap[at, :]

        def shaped(x, taps):
            total = taps[:, 0:1] * x
            for j in range(1, TAPS):
                total = total + taps[:, j : j + 1] * pltpu.roll(x, j, 1)
            return total

        size = k.shape[1]
        o_ref[at, :size] = (shaped(k, kt) * shaped(v, vt)).astype(BF16)

        def edges(x, by):
            ends = jnp.where(lane >= LANES - EDGE, x[:, size - LANES :], x[:, :LANES])
            return pltpu.roll(ends, by, 1)

        o_ref[at, size:] = jnp.where(
            lane < LANES // 2, edges(k, EDGE), edges(v, EDGE + LANES // 2)
        ).astype(BF16)
        return carry

    lax.fori_loop(0, GATE_ROWS // STEP, step, 0, unroll=2)


def gate_call(features, short_taps):
    _, channels, size = features.shape
    return pl.pallas_call(
        gate_kernel,
        grid=(channels // GATE_ROWS,),
        in_specs=[
            pl.BlockSpec(short_taps.shape, lambda g: (0, 0, 0)),
            pl.BlockSpec((1, GATE_ROWS, size), lambda g: (1, g, 0)),
            pl.BlockSpec((1, GATE_ROWS, size), lambda g: (2, g, 0)),
        ],
        out_specs=pl.BlockSpec((GATE_ROWS, size + LANES), lambda g: (g, 0)),
        out_shape=jax.ShapeDtypeStruct((channels, size + LANES), BF16),
        scratch_shapes=[pltpu.VMEM((GATE_ROWS, 8), F32)] * 2,
        cost_estimate=pl.CostEstimate(flops=60 * channels * size, bytes_accessed=6 * channels * size, transcendentals=0),
        name="gate",
    )(short_taps, features, features)


def query_kernel(taps_ref, halo_ref, q_ref, o_ref, qtap, before):
    start = pl.multiple_of(pl.program_id(0) * GATE_ROWS, GATE_ROWS)
    qtap[...] = tap_columns(taps_ref, 0, start, GATE_ROWS)
    halo = halo_ref[...].astype(F32)
    before[...] = jnp.concatenate([jnp.zeros((LANES - EDGE, GATE_ROWS), F32), halo], 0).T

    def step(g, carry):
        at = pl.ds(pl.multiple_of(g * STEP, STEP), STEP)
        x = jnp.concatenate([before[at, :], q_ref[0, at, :].astype(F32)], 1)
        taps = qtap[at, :]
        total = taps[:, 0:1] * x[:, LANES:]
        for j in range(1, TAPS):
            total = total + taps[:, j : j + 1] * pltpu.roll(x, j, 1)[:, LANES:]
        o_ref[at, :] = total
        return carry

    lax.fori_loop(0, GATE_ROWS // STEP, step, 0)


def query_call(features, short_taps, halo):
    _, channels, size = features.shape
    return pl.pallas_call(
        query_kernel,
        grid=(channels // GATE_ROWS,),
        in_specs=[
            pl.BlockSpec(short_taps.shape, lambda g: (0, 0, 0)),
            pl.BlockSpec((EDGE, GATE_ROWS), lambda g: (0, g)),
            pl.BlockSpec((1, GATE_ROWS, size), lambda g: (0, g, 0)),
        ],
        out_specs=pl.BlockSpec((GATE_ROWS, size), lambda g: (g, 0)),
        out_shape=jax.ShapeDtypeStruct((channels, size), F32),
        scratch_shapes=[pltpu.VMEM((GATE_ROWS, 8), F32), pltpu.VMEM((GATE_ROWS, LANES), F32)],
        cost_estimate=pl.CostEstimate(flops=30 * channels * size, bytes_accessed=6 * channels * size, transcendentals=0),
        name="query",
    )(short_taps, halo, features)


def filter_kernel(place_ref, skip_ref, f_ref, rhi, rlo, twr, twi, fhi, flo, o_ref, grid_ref):
    own = f_ref.shape[0]
    for j in range(N1):
        grid_ref[j * own : (j + 1) * own, :] = f_ref[:, j * N2 : (j + 1) * N2]

    def pair(c, carry):
        x = jnp.concatenate([grid_ref[pl.ds(2 * c + a, N1, stride=own), :] for a in range(2)], 1)
        hi, lo = split(x)
        part = mm(rhi[...], hi) + mm(rlo[...], hi) + mm(rhi[...], lo)
        re, im = part[:N1], part[N1:]
        tr, ti = twice(twr[...]), twice(twi[...])
        turned_re, turned_im = re * tr - im * ti, re * ti + im * tr
        for a in range(2):
            at = slice(a * N2, (a + 1) * N2)
            spec = mm3(jnp.concatenate([turned_re[:, at], turned_im[:, at]], 1), fhi[...], flo[...])
            skip = skip_ref[place_ref[1] + 2 * c + a]
            o_ref[2 * c + a, :, :N2] = (spec[:, :N2] + skip) * (1.0 / TOTAL)
            o_ref[2 * c + a, :, N2:] = spec[:, N2:] * (1.0 / TOTAL)
        return carry

    lax.fori_loop(0, own // 2, pair, 0)


def whole(x):
    return pl.BlockSpec(x.shape, lambda *_: (0,) * x.ndim)


def filter_call(filters, skip, half_place, first_channel, own, tables):
    consts = [*tables["rows"], *tables["twist"], *tables["forward"]]
    return pl.pallas_call(
        filter_kernel,
        grid_spec=pltpu.PrefetchScalarGridSpec(
            num_scalar_prefetch=1,
            grid=(1,),
            in_specs=[
                pl.BlockSpec(memory_space=pltpu.SMEM),
                pl.BlockSpec((own, filters.shape[1]), lambda g, place: (place[0], 0)),
                *[whole(c) for c in consts],
            ],
            out_specs=pl.BlockSpec((own, N1, 2 * N2), lambda g, place: (0, 0, 0)),
            scratch_shapes=[pltpu.VMEM((N1 * own, N2), F32)],
        ),
        out_shape=jax.ShapeDtypeStruct((own, N1, 2 * N2), F32),
        compiler_params=pltpu.CompilerParams(vmem_limit_bytes=32 * 1024 * 1024),
        cost_estimate=pl.CostEstimate(flops=12 * own * N1 * N1 * 2 * N2, bytes_accessed=4 << 20, transcendentals=0),
        name="filter_spectrum",
    )(jnp.stack([half_place, first_channel]).astype(jnp.int32), skip, filters, *consts)


def conv_kernel(x_ref, h_ref, taps_ref, rhi, rlo, twr, twi, fhi, flo, bhi, blo, chi, clo, o_ref, grid_ref, edge_ref, res_ref):
    own = h_ref.shape[0]
    blocks = x_ref.shape[0] // own
    size = x_ref.shape[1] - LANES
    tiles = size // LANES
    pairs = blocks // 2

    def unpack(i, carry):
        rows = pl.ds(pl.multiple_of(i * 2 * own, 2 * own), 2 * own)
        for q in range(tiles + 1):
            tile = x_ref[rows, q * LANES : (q + 1) * LANES].astype(F32)
            for h in range(2):
                place = i + h * pairs
                if q < tiles:
                    at, to = place * tiles + q, grid_ref
                else:
                    at, to = place, edge_ref
                to[pl.ds(pl.multiple_of(at * own, own), own), :] = tile[h * own : (h + 1) * own]
        return carry

    lax.fori_loop(0, pairs, unpack, 0, unroll=4)

    lane = lax.broadcasted_iota(jnp.int32, (own, LANES), 1)

    def mend(p, carry):
        here = edge_ref[pl.ds(pl.multiple_of(p * own, own), own), :]
        previous = edge_ref[pl.ds(pl.multiple_of(jnp.maximum(p - 1, 0) * own, own), own), :]
        previous = jnp.where(p > 0, previous, 0.0)
        both = jnp.where(lane % (LANES // 2) < EDGE, previous, here)
        total = taps_ref[0] * both
        for j in range(1, TAPS):
            total = total + taps_ref[j] * pltpu.roll(both, j, 1)
        gated = pltpu.roll(total * pltpu.roll(total, LANES // 2, 1), LANES - EDGE, 1)
        at = pl.ds(pl.multiple_of(p * tiles * own, own), own)
        grid_ref[at, :] = jnp.where(lane < EDGE, gated, grid_ref[at, :])
        return carry

    lax.fori_loop(0, blocks, mend, 0, unroll=8)

    def pair(c, carry):
        x = jnp.concatenate([grid_ref[pl.ds(2 * c + a, N1, stride=own), :] for a in range(2)], 1).astype(BF16)
        part = mm(rhi[...], x) + mm(rlo[...], x)
        re, im = part[:N1], part[N1:]
        tr, ti = twice(twr[...]), twice(twi[...])
        turned_re, turned_im = re * tr - im * ti, re * ti + im * tr
        back_re, back_im = [], []
        for a in range(2):
            at = slice(a * N2, (a + 1) * N2)
            spec = mm3(jnp.concatenate([turned_re[:, at], turned_im[:, at]], 1), fhi[...], flo[...])
            sr, si = spec[:, :N2], spec[:, N2:]
            hr, hi = h_ref[2 * c + a, :, :N2], h_ref[2 * c + a, :, N2:]
            mid = mm3(jnp.concatenate([sr * hr - si * hi, sr * hi + si * hr], 1), bhi[...], blo[...])
            mr, mi = mid[:, :N2], mid[:, N2:]
            back_re.append(mr * twr[...] + mi * twi[...])
            back_im.append(mi * twr[...] - mr * twi[...])
        back = jnp.concatenate([jnp.concatenate(back_re, 1), jnp.concatenate(back_im, 1)], 0)
        hi, lo = split(back)
        y = mm(chi[...], hi) + mm(chi[...], lo) + mm(clo[...], hi)
        for a in range(2):
            res_ref[pl.ds(2 * c + a, N1, stride=own), :] = y[:, a * N2 : (a + 1) * N2]
        return carry

    lax.fori_loop(0, own // 2, pair, 0)

    def pack(i, carry):
        rows = pl.ds(pl.multiple_of(i * 2 * own, 2 * own), 2 * own)
        for q in range(tiles):
            tile = [
                res_ref[pl.ds(pl.multiple_of(((i + h * pairs) * tiles + q) * own, own), own), :] for h in range(2)
            ]
            o_ref[rows, q * LANES : (q + 1) * LANES] = jnp.concatenate(tile, 0).astype(BF16)
        return carry

    lax.fori_loop(0, pairs, pack, 0, unroll=4)


def conv_call(blocks, spectrum, taps, tables):
    own = spectrum.shape[0]
    rows, width = blocks.shape
    args = [
        blocks, spectrum, taps, *tables["rows"], *tables["twist"], *tables["forward"], *tables["backward"],
        *tables["back_rows"],
    ]
    return pl.pallas_call(
        conv_kernel,
        grid=(1,),
        in_specs=[whole(a) for a in args],
        out_specs=pl.BlockSpec((rows, width - LANES), lambda g: (0, 0)),
        out_shape=jax.ShapeDtypeStruct((rows, width - LANES), BF16),
        scratch_shapes=[
            pltpu.VMEM((N1 * own, N2), F32),
            pltpu.VMEM((rows, LANES), F32),
            pltpu.VMEM((N1 * own, N2), F32),
        ],
        compiler_params=pltpu.CompilerParams(vmem_limit_bytes=40 * 1024 * 1024),
        cost_estimate=pl.CostEstimate(flops=22 * own * N1 * N1 * 2 * N2, bytes_accessed=6 << 20, transcendentals=0),
        name="long_convolution",
    )(*args)


def shards(features, short_taps, filters, skip):
    size = features.shape[2]
    positions = lax.axis_size("half") * lax.axis_size("ctx")
    own = filters.shape[0] // lax.axis_size("half")
    half_place, ctx_place = lax.axis_index("half"), lax.axis_index("ctx")
    first_channel = ctx_place * filters.shape[0] + half_place * own
    tables = transform_tables()

    gated = gate_call(features, short_taps)
    blocks = lax.all_to_all(gated, ("ctx", "half"), 0, 0, tiled=True)

    tail = features[0, :, size - EDGE :].T
    halo = lax.ppermute(tail, ("half", "ctx"), [(i, i + 1) for i in range(positions - 1)])
    query = query_call(features, short_taps, halo)
    spectrum = filter_call(filters, skip, half_place, first_channel, own, tables)
    own_taps = lax.dynamic_slice_in_dim(short_taps[:, 1:], first_channel, own, 2)
    own_taps = jnp.repeat(jnp.swapaxes(own_taps, 1, 2), LANES // 2, axis=2)

    convolved = conv_call(blocks, spectrum, own_taps, tables)
    back = lax.all_to_all(convolved, ("ctx", "half"), 0, 0, tiled=True)
    return (query * back.astype(F32)).astype(BF16)


def solution(mesh):
    in_specs = (P("seq", None, ("half", "ctx")), P(), P("ctx", None), P())
    out_specs = P("seq", ("half", "ctx"))
    return jax.shard_map(shards, mesh=mesh, in_specs=in_specs, out_specs=out_specs, check_vma=False)
```

```python
import math

import jax
import jax.numpy as jnp
import ml_dtypes
import numpy as np
from jax import lax
from jax.experimental import pallas as pl
from jax.experimental.pallas import tpu as pltpu
from jax.sharding import PartitionSpec as P

TAPS = 7
EDGE = TAPS - 1
LANES = 128
N1 = 256
N2 = 128
TOTAL = N1 * N2
F32 = jnp.float32
BF16 = jnp.bfloat16


def halves(table):
    hi = table.astype(ml_dtypes.bfloat16)
    lo = (table - hi.astype(np.float64)).astype(ml_dtypes.bfloat16)
    return hi, lo


def transform_tables():
    k1 = np.arange(N1) + 0.25
    first = np.exp(-2j * np.pi * np.outer(k1, np.arange(N1)) / N1)
    twist = np.exp(-2j * np.pi * np.outer(k1, np.arange(N2)) / TOTAL)
    second = np.exp(-2j * np.pi * np.outer(np.arange(N2), np.arange(N2)) / N2)
    rows = np.concatenate([first.real, first.imag], 0)
    columns = np.block([[second.real, second.imag], [-second.imag, second.real]])
    back = np.concatenate([first.real.T, -first.imag.T], 0)
    table = np.concatenate([*halves(rows), *halves(columns), *halves(back)], 0)
    return jnp.asarray(table), jnp.asarray(np.concatenate([twist.real, twist.imag], 0).astype(np.float32))


ROWS = slice(0, 4 * N1)
COLS_HI, COLS_LO = slice(4 * N1, 5 * N1), slice(5 * N1, 6 * N1)
BACK = 6 * N1
FORWARD = slice(0, BACK)
VMEM_LIMIT = 60 * 1024 * 1024
CONV_LIMIT = 54525952


def mm(a, b):
    return jnp.dot(a, b, preferred_element_type=F32)


def split(x):
    hi = x.astype(BF16)
    return hi, (x - hi.astype(F32)).astype(BF16)


def mm3(x, whi, wlo):
    hi, lo = split(x)
    return mm(hi, whi) + mm(lo, whi) + mm(hi, wlo)


def rows_at(i, count):
    return pl.ds(pl.multiple_of(i * count, count), count)


STEP = 256


def fill_selectors(shift_ref, spread_ref):
    shape = shift_ref.shape
    row, col = lax.broadcasted_iota(jnp.int32, shape, 0), lax.broadcasted_iota(jnp.int32, shape, 1)
    shift_ref[...] = jnp.where(row == LANES + col % LANES - (col // LANES + 1), 1.0, 0.0).astype(BF16)
    shape = spread_ref.shape
    row, col = lax.broadcasted_iota(jnp.int32, shape, 0), lax.broadcasted_iota(jnp.int32, shape, 1)
    spread_ref[...] = jnp.where((row < 24) & (row % 8 == col // LANES), 1.0, 0.0).astype(BF16)


def spread_taps(taps_ref, branch, start, spread):
    taps = jnp.concatenate([taps_ref[branch, :, pl.ds(start, STEP)], jnp.zeros((1, STEP), F32)], 0)
    hi = taps.astype(BF16).astype(F32)
    mid = (taps - hi).astype(BF16).astype(F32)
    columns = jnp.concatenate([hi, mid, taps - hi - mid, jnp.zeros((LANES - 24, STEP), F32)], 0).T
    return mm(columns.astype(BF16), spread)


def shaped_tile(previous, current, taps, shift):
    moved = mm(jnp.concatenate([previous, current], 1), shift)
    total = taps[:, :LANES] * current.astype(F32)
    for j in range(1, TAPS):
        total = total + taps[:, j * LANES : (j + 1) * LANES] * moved[:, (j - 1) * LANES : j * LANES]
    return total


def gate_kernel(taps_ref, k_ref, v_ref, o_ref, shift, spread, ktaps, vtaps):
    @pl.when(pl.program_id(0) == 0)
    def _():
        fill_selectors(shift, spread)

    start = pl.multiple_of(pl.program_id(0) * STEP, STEP)
    size = k_ref.shape[2]
    tiles = size // LANES
    ktaps[...] = spread_taps(taps_ref, 1, start, spread[...])
    vtaps[...] = spread_taps(taps_ref, 2, start, spread[...])

    def tile(ref, q):
        return ref[0, :, q * LANES : (q + 1) * LANES]

    for q in range(tiles):
        key = shaped_tile(tile(k_ref, (q - 1) % tiles), tile(k_ref, q), ktaps[...], shift[...])
        value = shaped_tile(tile(v_ref, (q - 1) % tiles), tile(v_ref, q), vtaps[...], shift[...])
        o_ref[:, q * LANES : (q + 1) * LANES] = (key * value).astype(BF16)
    lane = lax.broadcasted_iota(jnp.int32, (STEP, LANES), 1)

    def edges(ref, by):
        ends = jnp.where(lane >= LANES - EDGE, tile(ref, tiles - 1).astype(F32), tile(ref, 0).astype(F32))
        return pltpu.roll(ends, by, 1)

    both = jnp.where(lane < LANES // 2, edges(k_ref, EDGE), edges(v_ref, EDGE + LANES // 2))
    o_ref[:, size:] = both.astype(BF16)


def short_scratch(count):
    return [
        pltpu.VMEM((2 * LANES, EDGE * LANES), BF16),
        pltpu.VMEM((LANES, TAPS * LANES), BF16),
        *[pltpu.VMEM((STEP, TAPS * LANES), F32)] * count,
    ]


def gate_call(features, taps):
    _, channels, size = features.shape
    return pl.pallas_call(
        gate_kernel,
        grid=(channels // STEP,),
        in_specs=[
            pl.BlockSpec(taps.shape, lambda g: (0, 0, 0)),
            pl.BlockSpec((1, STEP, size), lambda g: (1, g, 0)),
            pl.BlockSpec((1, STEP, size), lambda g: (2, g, 0)),
        ],
        out_specs=pl.BlockSpec((STEP, size + LANES), lambda g: (g, 0)),
        out_shape=jax.ShapeDtypeStruct((channels, size + LANES), BF16),
        scratch_shapes=short_scratch(2),
        compiler_params=pltpu.CompilerParams(vmem_limit_bytes=VMEM_LIMIT),
        cost_estimate=pl.CostEstimate(flops=60 * channels * size, bytes_accessed=6 * channels * size, transcendentals=0),
        name="gate",
    )(taps, features, features)


def query_kernel(taps_ref, halo_ref, q_ref, o_ref, shift, spread, qtaps):
    @pl.when(pl.program_id(0) == 0)
    def _():
        fill_selectors(shift, spread)

    start = pl.multiple_of(pl.program_id(0) * STEP, STEP)
    qtaps[...] = spread_taps(taps_ref, 0, start, spread[...])
    halo = halo_ref[...].astype(F32)
    previous = jnp.concatenate([jnp.zeros((LANES - EDGE, STEP), F32), halo], 0).T.astype(BF16)
    for q in range(q_ref.shape[2] // LANES):
        current = q_ref[0, :, q * LANES : (q + 1) * LANES]
        o_ref[:, q * LANES : (q + 1) * LANES] = shaped_tile(previous, current, qtaps[...], shift[...])
        previous = current


def query_call(features, taps, halo):
    _, channels, size = features.shape
    return pl.pallas_call(
        query_kernel,
        grid=(channels // STEP,),
        in_specs=[
            pl.BlockSpec(taps.shape, lambda g: (0, 0, 0)),
            pl.BlockSpec((EDGE, STEP), lambda g: (0, g)),
            pl.BlockSpec((1, STEP, size), lambda g: (0, g, 0)),
        ],
        out_specs=pl.BlockSpec((STEP, size), lambda g: (g, 0)),
        out_shape=jax.ShapeDtypeStruct((channels, size), F32),
        scratch_shapes=short_scratch(1),
        cost_estimate=pl.CostEstimate(flops=30 * channels * size, bytes_accessed=6 * channels * size, transcendentals=0),
        name="query",
    )(taps, halo, features)


ANY = pl.BlockSpec(memory_space=pl.ANY)


def pair_of(grid_ref, c, own):
    return jnp.concatenate([grid_ref[pl.ds(2 * c + a, N1, stride=own), :] for a in range(2)], 1)


def filter_kernel(place_ref, skip_ref, f_ref, table_any, twist_ref, o_ref, grid_ref, table, sem):
    copy = pltpu.make_async_copy(table_any.at[FORWARD, :], table, sem)
    copy.start()
    own = f_ref.shape[0]
    for j in range(N1):
        grid_ref[j * own : (j + 1) * own, :] = f_ref[:, j * N2 : (j + 1) * N2]
    copy.wait()

    def pair(c, carry):
        hi, lo = split(pair_of(grid_ref, c, own))
        top, low = table[: 2 * N1], table[2 * N1 : 4 * N1]
        part = mm(top, hi) + mm(low, hi) + mm(top, lo)
        twr, twi = twist_ref[:N1], twist_ref[N1:]
        for a in range(2):
            re, im = part[:N1, a * N2 : (a + 1) * N2], part[N1:, a * N2 : (a + 1) * N2]
            turned = jnp.concatenate([re * twr - im * twi, re * twi + im * twr], 1)
            spec = mm3(turned, table[COLS_HI], table[COLS_LO])
            skip = skip_ref[place_ref[1] + 2 * c + a]
            o_ref[2 * c + a, :, :N2] = (spec[:, :N2] + skip) * (1.0 / TOTAL)
            o_ref[2 * c + a, :, N2:] = spec[:, N2:] * (-1.0 / TOTAL)
        return carry

    lax.fori_loop(0, own // 2, pair, 0)


def filter_call(filters, skip, half_place, first_channel, own, table, twist):
    return pl.pallas_call(
        filter_kernel,
        grid_spec=pltpu.PrefetchScalarGridSpec(
            num_scalar_prefetch=1,
            grid=(1,),
            in_specs=[
                pl.BlockSpec(memory_space=pltpu.SMEM),
                pl.BlockSpec((own, filters.shape[1]), lambda g, place: (place[0], 0)),
                ANY,
                pl.BlockSpec(twist.shape, lambda g, place: (0, 0)),
            ],
            out_specs=pl.BlockSpec((own, N1, 2 * N2), lambda g, place: (0, 0, 0)),
            scratch_shapes=[pltpu.VMEM((N1 * own, N2), F32), pltpu.VMEM((BACK, N1), BF16), pltpu.SemaphoreType.DMA],
        ),
        out_shape=jax.ShapeDtypeStruct((own, N1, 2 * N2), F32),
        compiler_params=pltpu.CompilerParams(vmem_limit_bytes=VMEM_LIMIT),
        cost_estimate=pl.CostEstimate(flops=12 * own * N1 * N1 * 2 * N2, bytes_accessed=6 << 20, transcendentals=0),
        name="filter_spectrum",
    )(jnp.stack([half_place, first_channel]).astype(jnp.int32), skip, filters, table, twist)


PIECES = 4


def conv_kernel(
    x_any, h_any, taps_ref, table_any, twist_any, o_any,
    grid_ref, edge_ref, res_ref, x_ref, h_ref, table, twist, o_ref, x_sem, h_sem, t_sem, o_sem,
):
    own = h_ref.shape[0]
    rows, width = x_ref.shape
    blocks = rows // own
    tiles = width // LANES - 1
    half = blocks // 2
    share = rows // PIECES
    x_copies = [
        pltpu.make_async_copy(x_any.at[pl.ds(i * share, share), :], x_ref.at[pl.ds(i * share, share), :], x_sem.at[i])
        for i in range(PIECES)
    ]
    cuts = [(0, 4 * N1), (4 * N1, 2 * N1), (6 * N1, 4 * N1)]
    t_copies = [
        pltpu.make_async_copy(table_any.at[pl.ds(at, n), :], table.at[pl.ds(at, n), :], t_sem.at[i])
        for i, (at, n) in enumerate(cuts)
    ]
    t_copies.insert(1, pltpu.make_async_copy(twist_any, twist, t_sem.at[len(cuts)]))
    h_copies = [
        pltpu.make_async_copy(h_any.at[pl.ds(2 * i, 2)], h_ref.at[pl.ds(2 * i, 2)], h_sem.at[i]) for i in range(own // 2)
    ]
    for copy in [*x_copies, *t_copies[:3], h_copies[0], t_copies[3], *h_copies[1:]]:
        copy.start()

    def unpack(i, carry):
        for q in range(tiles + 1):
            tile = x_ref[rows_at(i, 2 * own), q * LANES : (q + 1) * LANES].astype(F32)
            for h in range(2):
                place = i + h * half
                if q < tiles:
                    grid_ref[rows_at(place * tiles + q, own), :] = tile[h * own : (h + 1) * own]
                else:
                    edge_ref[rows_at(place, own), :] = tile[h * own : (h + 1) * own]
        return carry

    per_piece = half // PIECES
    for i in range(PIECES):
        x_copies[i].wait()
        lax.fori_loop(i * per_piece, (i + 1) * per_piece, unpack, 0, unroll=4)

    lane = lax.broadcasted_iota(jnp.int32, (own, LANES), 1)

    def mend(p, carry):
        here = edge_ref[rows_at(p, own), :]
        previous = jnp.where(p > 0, edge_ref[rows_at(jnp.maximum(p - 1, 0), own), :], 0.0)
        both = jnp.where(lane % (LANES // 2) < EDGE, previous, here)
        total = taps_ref[0] * both
        for j in range(1, TAPS):
            total = total + taps_ref[j] * pltpu.roll(both, j, 1)
        gated = pltpu.roll(total * pltpu.roll(total, LANES // 2, 1), LANES - EDGE, 1)
        at = rows_at(p * tiles, own)
        grid_ref[at, :] = jnp.where(lane < EDGE, gated, grid_ref[at, :])
        return carry

    lax.fori_loop(0, blocks, mend, 0, unroll=8)
    for copy in t_copies[:3]:
        copy.wait()

    for c in range(own // 2):
        x = pair_of(grid_ref, c, own).astype(BF16)
        part = mm(table[: 2 * N1], x) + mm(table[2 * N1 : 4 * N1], x)
        twr, twi = twist[:N1], twist[N1:]
        back_re, back_im = [], []
        h_copies[c].wait()
        for a in range(2):
            re, im = part[:N1, a * N2 : (a + 1) * N2], part[N1:, a * N2 : (a + 1) * N2]
            turned = jnp.concatenate([re * twr - im * twi, re * twi + im * twr], 1)
            spec = mm3(turned, table[COLS_HI], table[COLS_LO])
            sr, si = spec[:, :N2], spec[:, N2:]
            hr, hi = h_ref[2 * c + a, :, :N2], h_ref[2 * c + a, :, N2:]
            mid = mm3(jnp.concatenate([sr * hr + si * hi, sr * hi - si * hr], 1), table[COLS_HI], table[COLS_LO])
            mr, mi = mid[:, :N2], mid[:, N2:]
            back_re.append(mr * twr - mi * twi)
            back_im.append(mi * twr + mr * twi)
        if c == 0:
            t_copies[3].wait()
        y = None
        for at, back in ((BACK, back_re), (BACK + N1, back_im)):
            hi, lo = split(jnp.concatenate(back, 1))
            top, low = table[at : at + N1], table[at + 2 * N1 : at + 3 * N1]
            term = mm(top, hi) + mm(top, lo) + mm(low, hi)
            y = term if y is None else y + term
        for a in range(2):
            res_ref[pl.ds(2 * c + a, N1, stride=own), :] = y[:, a * N2 : (a + 1) * N2]

    def pack(i, carry):
        for q in range(tiles):
            tile = [res_ref[rows_at((i + h * half) * tiles + q, own), :] for h in range(2)]
            o_ref[rows_at(i, 2 * own), q * LANES : (q + 1) * LANES] = jnp.concatenate(tile, 0).astype(BF16)
        return carry

    o_copies = []
    for i in range(PIECES):
        lax.fori_loop(i * per_piece, (i + 1) * per_piece, pack, 0, unroll=4)
        piece = pl.ds(i * share, share)
        o_copies.append(pltpu.make_async_copy(o_ref.at[piece, :], o_any.at[piece, :], o_sem.at[i]))
        o_copies[-1].start()
    for copy in o_copies:
        copy.wait()


def conv_call(blocks, spectrum, taps, table, twist):
    own = spectrum.shape[0]
    rows, width = blocks.shape
    out = (rows, width - LANES)
    return pl.pallas_call(
        conv_kernel,
        in_specs=[ANY, ANY, pl.BlockSpec(memory_space=pltpu.VMEM), ANY, ANY],
        out_specs=ANY,
        out_shape=jax.ShapeDtypeStruct(out, BF16),
        scratch_shapes=[
            pltpu.VMEM((N1 * own, N2), F32),
            pltpu.VMEM((rows, LANES), F32),
            pltpu.VMEM((N1 * own, N2), F32),
            pltpu.VMEM(blocks.shape, BF16),
            pltpu.VMEM(spectrum.shape, F32),
            pltpu.VMEM(table.shape, BF16),
            pltpu.VMEM(twist.shape, F32),
            pltpu.VMEM(out, BF16),
            pltpu.SemaphoreType.DMA((PIECES,)),
            pltpu.SemaphoreType.DMA((own // 2,)),
            pltpu.SemaphoreType.DMA((4,)),
            pltpu.SemaphoreType.DMA((PIECES,)),
        ],
        compiler_params=pltpu.CompilerParams(vmem_limit_bytes=CONV_LIMIT),
        cost_estimate=pl.CostEstimate(flops=22 * own * N1 * N1 * 2 * N2, bytes_accessed=6 << 20, transcendentals=0),
        name="long_convolution",
    )(blocks, spectrum, taps, table, twist)


def shards(features, short_taps, filters, skip):
    size = features.shape[2]
    positions = lax.axis_size("half") * lax.axis_size("ctx")
    own = filters.shape[0] // lax.axis_size("half")
    half_place, ctx_place = lax.axis_index("half"), lax.axis_index("ctx")
    first_channel = ctx_place * filters.shape[0] + half_place * own
    table, twist = transform_tables()
    taps = jnp.swapaxes(short_taps, 0, 1)

    gated = gate_call(features, taps)
    blocks = lax.all_to_all(gated, ("ctx", "half"), 0, 0, tiled=True)

    tail = features[0, :, size - EDGE :].T
    halo = lax.ppermute(tail, ("half", "ctx"), [(i, i + 1) for i in range(positions - 1)])
    spectrum = filter_call(filters, skip, half_place, first_channel, own, table, twist)
    own_taps = lax.dynamic_slice_in_dim(taps[1:], first_channel, own, 2)
    own_taps = jnp.repeat(own_taps.transpose(1, 2, 0), LANES // 2, axis=2)
    halo, spectrum = lax.optimization_barrier((halo, spectrum))

    convolved = conv_call(blocks, spectrum, own_taps, table, twist)
    back = lax.all_to_all(convolved, ("ctx", "half"), 0, 0, tiled=True)
    query = query_call(features, taps, halo)
    return (query * back.astype(F32)).astype(BF16)


def solution(mesh):
    in_specs = (P("seq", None, ("half", "ctx")), P(), P("ctx", None), P())
    out_specs = P("seq", ("half", "ctx"))
    return jax.shard_map(shards, mesh=mesh, in_specs=in_specs, out_specs=out_specs, check_vma=False)
```

```python
import math

import jax
import jax.numpy as jnp
import ml_dtypes
import numpy as np
from jax import lax
from jax.experimental import pallas as pl
from jax.experimental.pallas import tpu as pltpu
from jax.sharding import PartitionSpec as P

TAPS = 7
EDGE = TAPS - 1
LANES = 128
N1 = 256
N2 = 128
TOTAL = N1 * N2
F32 = jnp.float32
BF16 = jnp.bfloat16


def halves(table):
    hi = table.astype(ml_dtypes.bfloat16)
    lo = (table - hi.astype(np.float64)).astype(ml_dtypes.bfloat16)
    return hi, lo


def transform_tables():
    k1 = np.arange(N1) + 0.25
    first = np.exp(-2j * np.pi * np.outer(k1, np.arange(N1)) / N1)
    twist = np.exp(-2j * np.pi * np.outer(k1, np.arange(N2)) / TOTAL)
    second = np.exp(-2j * np.pi * np.outer(np.arange(N2), np.arange(N2)) / N2)
    rows = np.concatenate([first.real, first.imag], 0)
    columns = np.block([[second.real, second.imag], [-second.imag, second.real]])
    back = np.concatenate([first.real.T, -first.imag.T], 0)
    gather, add = np.zeros((LANES, 2 * LANES)), np.zeros((LANES, 2 * LANES))
    for branch in range(2):
        for j in range(TAPS):
            for t in range(EDGE):
                at = branch * LANES // 2 + j * 8 + t
                gather[branch * LANES // 2 + EDGE + t - j, at] = 1
                add[at, branch * LANES + t] = 1
    exact = [gather.astype(ml_dtypes.bfloat16), add.astype(ml_dtypes.bfloat16)]
    table = np.concatenate([*halves(rows), *halves(columns), *halves(back), *exact], 0)
    return jnp.asarray(table), jnp.asarray(np.concatenate([twist.real, twist.imag], 0).astype(np.float32))


ROWS = slice(0, 4 * N1)
COLS_HI, COLS_LO = slice(4 * N1, 5 * N1), slice(5 * N1, 6 * N1)
BACK = 6 * N1
GATHER = 10 * N1
FORWARD = slice(0, BACK)
VMEM_LIMIT = 60 * 1024 * 1024
CONV_LIMIT = 54525952


def mm(a, b):
    return jnp.dot(a, b, preferred_element_type=F32)


def split(x):
    hi = x.astype(BF16)
    return hi, (x - hi.astype(F32)).astype(BF16)


def mm3(x, whi, wlo):
    hi, lo = split(x)
    return mm(hi, whi) + mm(lo, whi) + mm(hi, wlo)


def rows_at(i, count):
    return pl.ds(pl.multiple_of(i * count, count), count)


STEP = 256


def fill_selectors(shift_ref, spread_ref):
    shape = shift_ref.shape
    row, col = lax.broadcasted_iota(jnp.int32, shape, 0), lax.broadcasted_iota(jnp.int32, shape, 1)
    shift_ref[...] = jnp.where(row == LANES + col % LANES - (col // LANES + 1), 1.0, 0.0).astype(BF16)
    shape = spread_ref.shape
    row, col = lax.broadcasted_iota(jnp.int32, shape, 0), lax.broadcasted_iota(jnp.int32, shape, 1)
    spread_ref[...] = jnp.where((row < 24) & (row % 8 == col // LANES), 1.0, 0.0).astype(BF16)


def spread_taps(taps_ref, branch, start, spread):
    taps = jnp.concatenate([taps_ref[branch, :, pl.ds(start, STEP)], jnp.zeros((1, STEP), F32)], 0)
    hi = taps.astype(BF16).astype(F32)
    mid = (taps - hi).astype(BF16).astype(F32)
    columns = jnp.concatenate([hi, mid, taps - hi - mid, jnp.zeros((LANES - 24, STEP), F32)], 0).T
    return mm(columns.astype(BF16), spread)


def shaped_tile(previous, current, taps, shift):
    moved = mm(jnp.concatenate([previous, current], 1), shift)
    total = taps[:, :LANES] * current.astype(F32)
    for j in range(1, TAPS):
        total = total + taps[:, j * LANES : (j + 1) * LANES] * moved[:, (j - 1) * LANES : j * LANES]
    return total


def gate_kernel(taps_ref, k_ref, v_ref, o_ref, shift, spread, ktaps, vtaps):
    @pl.when(pl.program_id(0) == 0)
    def _():
        fill_selectors(shift, spread)

    start = pl.multiple_of(pl.program_id(0) * STEP, STEP)
    size = k_ref.shape[2]
    tiles = size // LANES
    ktaps[...] = spread_taps(taps_ref, 1, start, spread[...])
    vtaps[...] = spread_taps(taps_ref, 2, start, spread[...])

    def tile(ref, q):
        return ref[0, :, q * LANES : (q + 1) * LANES]

    for q in range(tiles):
        key = shaped_tile(tile(k_ref, (q - 1) % tiles), tile(k_ref, q), ktaps[...], shift[...])
        value = shaped_tile(tile(v_ref, (q - 1) % tiles), tile(v_ref, q), vtaps[...], shift[...])
        o_ref[:, q * LANES : (q + 1) * LANES] = (key * value).astype(BF16)
    lane = lax.broadcasted_iota(jnp.int32, (STEP, LANES), 1)

    def edges(ref, by):
        ends = jnp.where(lane >= LANES - EDGE, tile(ref, tiles - 1).astype(F32), tile(ref, 0).astype(F32))
        return pltpu.roll(ends, by, 1)

    both = jnp.where(lane < LANES // 2, edges(k_ref, EDGE), edges(v_ref, EDGE + LANES // 2))
    o_ref[:, size:] = both.astype(BF16)


def short_scratch(count):
    return [
        pltpu.VMEM((2 * LANES, EDGE * LANES), BF16),
        pltpu.VMEM((LANES, TAPS * LANES), BF16),
        *[pltpu.VMEM((STEP, TAPS * LANES), F32)] * count,
    ]


def gate_call(features, taps):
    _, channels, size = features.shape
    return pl.pallas_call(
        gate_kernel,
        grid=(channels // STEP,),
        in_specs=[
            pl.BlockSpec(taps.shape, lambda g: (0, 0, 0)),
            pl.BlockSpec((1, STEP, size), lambda g: (1, g, 0)),
            pl.BlockSpec((1, STEP, size), lambda g: (2, g, 0)),
        ],
        out_specs=pl.BlockSpec((STEP, size + LANES), lambda g: (g, 0)),
        out_shape=jax.ShapeDtypeStruct((channels, size + LANES), BF16),
        scratch_shapes=short_scratch(2),
        compiler_params=pltpu.CompilerParams(vmem_limit_bytes=VMEM_LIMIT),
        cost_estimate=pl.CostEstimate(flops=60 * channels * size, bytes_accessed=6 * channels * size, transcendentals=0),
        name="gate",
    )(taps, features, features)


def query_kernel(taps_ref, halo_ref, q_ref, o_ref, shift, spread, qtaps):
    @pl.when(pl.program_id(0) == 0)
    def _():
        fill_selectors(shift, spread)

    start = pl.multiple_of(pl.program_id(0) * STEP, STEP)
    qtaps[...] = spread_taps(taps_ref, 0, start, spread[...])
    halo = halo_ref[...].astype(F32)
    previous = jnp.concatenate([jnp.zeros((LANES - EDGE, STEP), F32), halo], 0).T.astype(BF16)
    for q in range(q_ref.shape[2] // LANES):
        current = q_ref[0, :, q * LANES : (q + 1) * LANES]
        o_ref[:, q * LANES : (q + 1) * LANES] = shaped_tile(previous, current, qtaps[...], shift[...])
        previous = current


def query_call(features, taps, halo):
    _, channels, size = features.shape
    return pl.pallas_call(
        query_kernel,
        grid=(channels // STEP,),
        in_specs=[
            pl.BlockSpec(taps.shape, lambda g: (0, 0, 0)),
            pl.BlockSpec((EDGE, STEP), lambda g: (0, g)),
            pl.BlockSpec((1, STEP, size), lambda g: (0, g, 0)),
        ],
        out_specs=pl.BlockSpec((STEP, size), lambda g: (g, 0)),
        out_shape=jax.ShapeDtypeStruct((channels, size), F32),
        scratch_shapes=short_scratch(1),
        cost_estimate=pl.CostEstimate(flops=30 * channels * size, bytes_accessed=6 * channels * size, transcendentals=0),
        name="query",
    )(taps, halo, features)


ANY = pl.BlockSpec(memory_space=pl.ANY)


def pair_of(grid_ref, c, own):
    return jnp.concatenate([grid_ref[pl.ds(2 * c + a, N1, stride=own), :] for a in range(2)], 1)


def filter_kernel(place_ref, skip_ref, f_ref, table_any, twist_ref, o_ref, grid_ref, table, sem):
    copy = pltpu.make_async_copy(table_any.at[FORWARD, :], table, sem)
    copy.start()
    own = f_ref.shape[0]
    for j in range(N1):
        grid_ref[j * own : (j + 1) * own, :] = f_ref[:, j * N2 : (j + 1) * N2]
    copy.wait()

    def pair(c, carry):
        hi, lo = split(pair_of(grid_ref, c, own))
        top, low = table[: 2 * N1], table[2 * N1 : 4 * N1]
        part = mm(top, hi) + mm(low, hi) + mm(top, lo)
        twr, twi = twist_ref[:N1], twist_ref[N1:]
        for a in range(2):
            re, im = part[:N1, a * N2 : (a + 1) * N2], part[N1:, a * N2 : (a + 1) * N2]
            turned = jnp.concatenate([re * twr - im * twi, re * twi + im * twr], 1)
            spec = mm3(turned, table[COLS_HI], table[COLS_LO])
            skip = skip_ref[place_ref[1] + 2 * c + a]
            o_ref[2 * c + a, :, :N2] = (spec[:, :N2] + skip) * (1.0 / TOTAL)
            o_ref[2 * c + a, :, N2:] = spec[:, N2:] * (-1.0 / TOTAL)
        return carry

    lax.fori_loop(0, own // 2, pair, 0)


def filter_call(filters, skip, half_place, first_channel, own, table, twist):
    return pl.pallas_call(
        filter_kernel,
        grid_spec=pltpu.PrefetchScalarGridSpec(
            num_scalar_prefetch=1,
            grid=(1,),
            in_specs=[
                pl.BlockSpec(memory_space=pltpu.SMEM),
                pl.BlockSpec((own, filters.shape[1]), lambda g, place: (place[0], 0)),
                ANY,
                pl.BlockSpec(twist.shape, lambda g, place: (0, 0)),
            ],
            out_specs=pl.BlockSpec((own, N1, 2 * N2), lambda g, place: (0, 0, 0)),
            scratch_shapes=[pltpu.VMEM((N1 * own, N2), F32), pltpu.VMEM((BACK, N1), BF16), pltpu.SemaphoreType.DMA],
        ),
        out_shape=jax.ShapeDtypeStruct((own, N1, 2 * N2), F32),
        compiler_params=pltpu.CompilerParams(vmem_limit_bytes=VMEM_LIMIT),
        cost_estimate=pl.CostEstimate(flops=12 * own * N1 * N1 * 2 * N2, bytes_accessed=6 << 20, transcendentals=0),
        name="filter_spectrum",
    )(jnp.stack([half_place, first_channel]).astype(jnp.int32), skip, filters, table, twist)


PIECES = 4


def conv_kernel(
    x_any, h_any, taps_ref, table_any, twist_any, o_any,
    grid_ref, edge_ref, res_ref, x_ref, h_ref, table, twist, o_ref, x_sem, h_sem, t_sem, o_sem,
):
    own = h_ref.shape[0]
    rows, width = x_ref.shape
    blocks = rows // own
    tiles = width // LANES - 1
    half = blocks // 2
    share = rows // PIECES
    x_copies = [
        pltpu.make_async_copy(x_any.at[pl.ds(i * share, share), :], x_ref.at[pl.ds(i * share, share), :], x_sem.at[i])
        for i in range(PIECES)
    ]
    cuts = [(0, 4 * N1), (4 * N1, 2 * N1), (BACK, 4 * N1), (GATHER, 2 * LANES)]
    t_copies = [
        pltpu.make_async_copy(table_any.at[pl.ds(at, n), :], table.at[pl.ds(at, n), :], t_sem.at[i])
        for i, (at, n) in enumerate(cuts)
    ]
    twist_copy = pltpu.make_async_copy(twist_any, twist, t_sem.at[len(cuts)])
    h_copies = [
        pltpu.make_async_copy(h_any.at[pl.ds(2 * i, 2)], h_ref.at[pl.ds(2 * i, 2)], h_sem.at[i]) for i in range(own // 2)
    ]
    for copy in [*x_copies, t_copies[3], t_copies[0], twist_copy, t_copies[1], *h_copies, t_copies[2]]:
        copy.start()

    def unpack(i, carry):
        for q in range(tiles + 1):
            tile = x_ref[rows_at(i, 2 * own), q * LANES : (q + 1) * LANES].astype(F32)
            for h in range(2):
                place = i + h * half
                if q < tiles:
                    grid_ref[rows_at(place * tiles + q, own), :] = tile[h * own : (h + 1) * own]
                else:
                    edge_ref[rows_at(place + 1, own), :] = tile[h * own : (h + 1) * own]
        return carry

    per_piece = half // PIECES
    for i in range(PIECES):
        x_copies[i].wait()
        lax.fori_loop(i * per_piece, (i + 1) * per_piece, unpack, 0, unroll=4)

    edge_ref[:own, :] = jnp.zeros((own, LANES), F32)
    lane = lax.broadcasted_iota(jnp.int32, (rows, LANES), 1)
    both = jnp.where(lane % (LANES // 2) < EDGE, edge_ref[:rows, :], edge_ref[own:, :]).astype(BF16)
    t_copies[3].wait()
    terms = mm(both, table[GATHER : GATHER + LANES, :LANES]).reshape(blocks, own, LANES) * taps_ref[...][None]
    hi, lo = split(terms.reshape(rows, LANES))
    add = table[GATHER + LANES : GATHER + 2 * LANES]
    sums = mm(hi, add) + mm(lo, add)
    gated = sums[:, :LANES] * sums[:, LANES:]
    for p in range(blocks):
        grid_ref[p * tiles * own : (p * tiles + 1) * own, :EDGE] = gated[p * own : (p + 1) * own, :EDGE]

    pairs = range(own // 2)
    t_copies[0].wait()
    twist_copy.wait()
    twr, twi = twist[:N1], twist[N1:]
    turned = []
    for c in pairs:
        x = pair_of(grid_ref, c, own).astype(BF16)
        part = mm(table[: 2 * N1], x) + mm(table[2 * N1 : 4 * N1], x)
        for a in range(2):
            re, im = part[:N1, a * N2 : (a + 1) * N2], part[N1:, a * N2 : (a + 1) * N2]
            turned.append(jnp.concatenate([re * twr - im * twi, re * twi + im * twr], 1))
    t_copies[1].wait()
    back = []
    for c in range(own):
        if c % 2 == 0:
            h_copies[c // 2].wait()
        spec = mm3(turned[c], table[COLS_HI], table[COLS_LO])
        sr, si = spec[:, :N2], spec[:, N2:]
        hr, hi = h_ref[c, :, :N2], h_ref[c, :, N2:]
        mid = mm3(jnp.concatenate([sr * hr + si * hi, sr * hi - si * hr], 1), table[COLS_HI], table[COLS_LO])
        mr, mi = mid[:, :N2], mid[:, N2:]
        back.append((mr * twr - mi * twi, mi * twr + mr * twi))
    t_copies[2].wait()
    for c in pairs:
        y = None
        for part in range(2):
            at = BACK + part * N1
            hi, lo = split(jnp.concatenate([back[2 * c][part], back[2 * c + 1][part]], 1))
            top, low = table[at : at + N1], table[at + 2 * N1 : at + 3 * N1]
            term = mm(top, hi) + mm(top, lo) + mm(low, hi)
            y = term if y is None else y + term
        for a in range(2):
            res_ref[pl.ds(2 * c + a, N1, stride=own), :] = y[:, a * N2 : (a + 1) * N2]

    def pack(i, carry):
        for q in range(tiles):
            tile = [res_ref[rows_at((i + h * half) * tiles + q, own), :] for h in range(2)]
            o_ref[rows_at(i, 2 * own), q * LANES : (q + 1) * LANES] = jnp.concatenate(tile, 0).astype(BF16)
        return carry

    o_copies = []
    for i in range(PIECES):
        lax.fori_loop(i * per_piece, (i + 1) * per_piece, pack, 0, unroll=4)
        piece = pl.ds(i * share, share)
        o_copies.append(pltpu.make_async_copy(o_ref.at[piece, :], o_any.at[piece, :], o_sem.at[i]))
        o_copies[-1].start()
    for copy in o_copies:
        copy.wait()


def conv_call(blocks, spectrum, taps, table, twist):
    own = spectrum.shape[0]
    rows, width = blocks.shape
    out = (rows, width - LANES)
    return pl.pallas_call(
        conv_kernel,
        in_specs=[ANY, ANY, pl.BlockSpec(memory_space=pltpu.VMEM), ANY, ANY],
        out_specs=ANY,
        out_shape=jax.ShapeDtypeStruct(out, BF16),
        scratch_shapes=[
            pltpu.VMEM((N1 * own, N2), F32),
            pltpu.VMEM((rows + own, LANES), F32),
            pltpu.VMEM((N1 * own, N2), F32),
            pltpu.VMEM(blocks.shape, BF16),
            pltpu.VMEM(spectrum.shape, F32),
            pltpu.VMEM(table.shape, BF16),
            pltpu.VMEM(twist.shape, F32),
            pltpu.VMEM(out, BF16),
            pltpu.SemaphoreType.DMA((PIECES,)),
            pltpu.SemaphoreType.DMA((own // 2,)),
            pltpu.SemaphoreType.DMA((5,)),
            pltpu.SemaphoreType.DMA((PIECES,)),
        ],
        compiler_params=pltpu.CompilerParams(vmem_limit_bytes=CONV_LIMIT),
        cost_estimate=pl.CostEstimate(flops=22 * own * N1 * N1 * 2 * N2, bytes_accessed=6 << 20, transcendentals=0),
        name="long_convolution",
    )(blocks, spectrum, taps, table, twist)


def shards(features, short_taps, filters, skip):
    size = features.shape[2]
    positions = lax.axis_size("half") * lax.axis_size("ctx")
    own = filters.shape[0] // lax.axis_size("half")
    half_place, ctx_place = lax.axis_index("half"), lax.axis_index("ctx")
    first_channel = ctx_place * filters.shape[0] + half_place * own
    table, twist = transform_tables()
    taps = jnp.swapaxes(short_taps, 0, 1)

    gated = gate_call(features, taps)
    blocks = lax.all_to_all(gated, ("ctx", "half"), 0, 0, tiled=True)

    tail = features[0, :, size - EDGE :].T
    halo = lax.ppermute(tail, ("half", "ctx"), [(i, i + 1) for i in range(positions - 1)])
    spectrum = filter_call(filters, skip, half_place, first_channel, own, table, twist)
    own_taps = lax.dynamic_slice_in_dim(taps[1:], first_channel, own, 2)
    own_taps = jnp.pad(own_taps.transpose(2, 0, 1), ((0, 0), (0, 0), (0, 8 - TAPS)))
    own_taps = jnp.repeat(own_taps.reshape(own, 16), 8, axis=1)
    halo, spectrum = lax.optimization_barrier((halo, spectrum))

    convolved = conv_call(blocks, spectrum, own_taps, table, twist)
    back = lax.all_to_all(convolved, ("ctx", "half"), 0, 0, tiled=True)
    query = query_call(features, taps, halo)
    return (query * back.astype(F32)).astype(BF16)


def solution(mesh):
    in_specs = (P("seq", None, ("half", "ctx")), P(), P("ctx", None), P())
    out_specs = P("seq", ("half", "ctx"))
    return jax.shard_map(shards, mesh=mesh, in_specs=in_specs, out_specs=out_specs, check_vma=False)
```

```python
import math

import jax
import jax.numpy as jnp
import ml_dtypes
import numpy as np
from jax import lax
from jax.experimental import pallas as pl
from jax.experimental.pallas import tpu as pltpu
from jax.sharding import PartitionSpec as P

TAPS = 7
EDGE = TAPS - 1
LANES = 128
N1 = 256
N2 = 128
TOTAL = N1 * N2
F32 = jnp.float32
BF16 = jnp.bfloat16


def halves(table):
    hi = table.astype(ml_dtypes.bfloat16)
    lo = (table - hi.astype(np.float64)).astype(ml_dtypes.bfloat16)
    return hi, lo


def transform_tables():
    k1 = np.arange(N1) + 0.25
    first = np.exp(-2j * np.pi * np.outer(k1, np.arange(N1)) / N1)
    twist = np.exp(-2j * np.pi * np.outer(k1, np.arange(N2)) / TOTAL)
    second = np.exp(-2j * np.pi * np.outer(np.arange(N2), np.arange(N2)) / N2)
    rows = np.concatenate([first.real, first.imag], 0)
    columns = np.block([[second.real, second.imag], [-second.imag, second.real]])
    back = np.concatenate([first.real.T, -first.imag.T], 0)
    gather, add = np.zeros((LANES, 2 * LANES)), np.zeros((LANES, 2 * LANES))
    for branch in range(2):
        for j in range(TAPS):
            for t in range(EDGE):
                at = branch * LANES // 2 + j * 8 + t
                gather[branch * LANES // 2 + EDGE + t - j, at] = 1
                add[at, branch * LANES + t] = 1
    exact = [gather.astype(ml_dtypes.bfloat16), add.astype(ml_dtypes.bfloat16)]
    table = np.concatenate([*halves(rows), *halves(columns), *halves(back), *exact], 0)
    return jnp.asarray(table), jnp.asarray(np.concatenate([twist.real, twist.imag], 0).astype(np.float32))


ROWS = slice(0, 4 * N1)
COLS_HI, COLS_LO = slice(4 * N1, 5 * N1), slice(5 * N1, 6 * N1)
BACK = 6 * N1
GATHER = 10 * N1
FORWARD = slice(0, BACK)
VMEM_LIMIT = 60 * 1024 * 1024
CONV_LIMIT = 54525952


def mm(a, b):
    return jnp.dot(a, b, preferred_element_type=F32)


def split(x):
    hi = x.astype(BF16)
    return hi, (x - hi.astype(F32)).astype(BF16)


def mm3(x, whi, wlo):
    hi, lo = split(x)
    return mm(hi, whi) + mm(lo, whi) + mm(hi, wlo)


def rows_at(i, count):
    return pl.ds(pl.multiple_of(i * count, count), count)


STEP = 256


def fill_selectors(shift_ref, spread_ref):
    shape = shift_ref.shape
    row, col = lax.broadcasted_iota(jnp.int32, shape, 0), lax.broadcasted_iota(jnp.int32, shape, 1)
    shift_ref[...] = jnp.where(row == LANES + col % LANES - (col // LANES + 1), 1.0, 0.0).astype(BF16)
    shape = spread_ref.shape
    row, col = lax.broadcasted_iota(jnp.int32, shape, 0), lax.broadcasted_iota(jnp.int32, shape, 1)
    spread_ref[...] = jnp.where((row < 24) & (row % 8 == col // LANES), 1.0, 0.0).astype(BF16)


def spread_taps(taps_ref, branch, start, spread):
    taps = jnp.concatenate([taps_ref[branch, :, pl.ds(start, STEP)], jnp.zeros((1, STEP), F32)], 0)
    hi = taps.astype(BF16).astype(F32)
    mid = (taps - hi).astype(BF16).astype(F32)
    columns = jnp.concatenate([hi, mid, taps - hi - mid, jnp.zeros((LANES - 24, STEP), F32)], 0).T
    return mm(columns.astype(BF16), spread)


def shaped_tile(previous, current, taps, shift):
    moved = mm(jnp.concatenate([previous, current], 1), shift)
    total = taps[:, :LANES] * current.astype(F32)
    for j in range(1, TAPS):
        total = total + taps[:, j * LANES : (j + 1) * LANES] * moved[:, (j - 1) * LANES : j * LANES]
    return total


def gate_kernel(taps_ref, k_ref, v_ref, o_ref, shift, spread, ktaps, vtaps):
    @pl.when(pl.program_id(0) == 0)
    def _():
        fill_selectors(shift, spread)

    start = pl.multiple_of(pl.program_id(0) * STEP, STEP)
    size = k_ref.shape[2]
    tiles = size // LANES
    ktaps[...] = spread_taps(taps_ref, 1, start, spread[...])
    vtaps[...] = spread_taps(taps_ref, 2, start, spread[...])

    def tile(ref, q):
        return ref[0, :, q * LANES : (q + 1) * LANES]

    for q in range(tiles):
        key = shaped_tile(tile(k_ref, (q - 1) % tiles), tile(k_ref, q), ktaps[...], shift[...])
        value = shaped_tile(tile(v_ref, (q - 1) % tiles), tile(v_ref, q), vtaps[...], shift[...])
        o_ref[:, q * LANES : (q + 1) * LANES] = (key * value).astype(BF16)
    lane = lax.broadcasted_iota(jnp.int32, (STEP, LANES), 1)

    def edges(ref, by):
        ends = jnp.where(lane >= LANES - EDGE, tile(ref, tiles - 1).astype(F32), tile(ref, 0).astype(F32))
        return pltpu.roll(ends, by, 1)

    both = jnp.where(lane < LANES // 2, edges(k_ref, EDGE), edges(v_ref, EDGE + LANES // 2))
    o_ref[:, size:] = both.astype(BF16)


def short_scratch(count):
    return [
        pltpu.VMEM((2 * LANES, EDGE * LANES), BF16),
        pltpu.VMEM((LANES, TAPS * LANES), BF16),
        *[pltpu.VMEM((STEP, TAPS * LANES), F32)] * count,
    ]


def gate_call(features, taps):
    _, channels, size = features.shape
    return pl.pallas_call(
        gate_kernel,
        grid=(channels // STEP,),
        in_specs=[
            pl.BlockSpec(taps.shape, lambda g: (0, 0, 0)),
            pl.BlockSpec((1, STEP, size), lambda g: (1, g, 0)),
            pl.BlockSpec((1, STEP, size), lambda g: (2, g, 0)),
        ],
        out_specs=pl.BlockSpec((STEP, size + LANES), lambda g: (g, 0)),
        out_shape=jax.ShapeDtypeStruct((channels, size + LANES), BF16),
        scratch_shapes=short_scratch(2),
        compiler_params=pltpu.CompilerParams(vmem_limit_bytes=VMEM_LIMIT),
        cost_estimate=pl.CostEstimate(flops=60 * channels * size, bytes_accessed=6 * channels * size, transcendentals=0),
        name="gate",
    )(taps, features, features)


def query_kernel(taps_ref, halo_ref, q_ref, o_ref, shift, spread, qtaps):
    @pl.when(pl.program_id(0) == 0)
    def _():
        fill_selectors(shift, spread)

    start = pl.multiple_of(pl.program_id(0) * STEP, STEP)
    qtaps[...] = spread_taps(taps_ref, 0, start, spread[...])
    halo = halo_ref[...].astype(F32)
    previous = jnp.concatenate([jnp.zeros((LANES - EDGE, STEP), F32), halo], 0).T.astype(BF16)
    for q in range(q_ref.shape[2] // LANES):
        current = q_ref[0, :, q * LANES : (q + 1) * LANES]
        o_ref[:, q * LANES : (q + 1) * LANES] = shaped_tile(previous, current, qtaps[...], shift[...])
        previous = current


def query_call(features, taps, halo):
    _, channels, size = features.shape
    return pl.pallas_call(
        query_kernel,
        grid=(channels // STEP,),
        in_specs=[
            pl.BlockSpec(taps.shape, lambda g: (0, 0, 0)),
            pl.BlockSpec((EDGE, STEP), lambda g: (0, g)),
            pl.BlockSpec((1, STEP, size), lambda g: (0, g, 0)),
        ],
        out_specs=pl.BlockSpec((STEP, size), lambda g: (g, 0)),
        out_shape=pltpu.VMEM((channels, size), F32),
        scratch_shapes=short_scratch(1),
        cost_estimate=pl.CostEstimate(flops=30 * channels * size, bytes_accessed=6 * channels * size, transcendentals=0),
        name="query",
    )(taps, halo, features)


ANY = pl.BlockSpec(memory_space=pl.ANY)


def pair_of(grid_ref, c, own):
    return jnp.concatenate([grid_ref[pl.ds(2 * c + a, N1, stride=own), :] for a in range(2)], 1)


def filter_kernel(place_ref, skip_ref, f_ref, table_any, twist_ref, o_ref, grid_ref, table, sem):
    copy = pltpu.make_async_copy(table_any.at[FORWARD, :], table, sem)
    copy.start()
    own = f_ref.shape[0]
    for j in range(N1):
        grid_ref[j * own : (j + 1) * own, :] = f_ref[:, j * N2 : (j + 1) * N2]
    copy.wait()

    def pair(c, carry):
        hi, lo = split(pair_of(grid_ref, c, own))
        top, low = table[: 2 * N1], table[2 * N1 : 4 * N1]
        part = mm(top, hi) + mm(low, hi) + mm(top, lo)
        twr, twi = twist_ref[:N1], twist_ref[N1:]
        for a in range(2):
            re, im = part[:N1, a * N2 : (a + 1) * N2], part[N1:, a * N2 : (a + 1) * N2]
            turned = jnp.concatenate([re * twr - im * twi, re * twi + im * twr], 1)
            spec = mm3(turned, table[COLS_HI], table[COLS_LO])
            skip = skip_ref[place_ref[1] + 2 * c + a]
            o_ref[2 * c + a, :, :N2] = (spec[:, :N2] + skip) * (1.0 / TOTAL)
            o_ref[2 * c + a, :, N2:] = spec[:, N2:] * (-1.0 / TOTAL)
        return carry

    lax.fori_loop(0, own // 2, pair, 0)


def filter_call(filters, skip, half_place, first_channel, own, table, twist):
    return pl.pallas_call(
        filter_kernel,
        grid_spec=pltpu.PrefetchScalarGridSpec(
            num_scalar_prefetch=1,
            grid=(1,),
            in_specs=[
                pl.BlockSpec(memory_space=pltpu.SMEM),
                pl.BlockSpec((own, filters.shape[1]), lambda g, place: (place[0], 0)),
                ANY,
                pl.BlockSpec(twist.shape, lambda g, place: (0, 0)),
            ],
            out_specs=pl.BlockSpec((own, N1, 2 * N2), lambda g, place: (0, 0, 0)),
            scratch_shapes=[pltpu.VMEM((N1 * own, N2), F32), pltpu.VMEM((BACK, N1), BF16), pltpu.SemaphoreType.DMA],
        ),
        out_shape=jax.ShapeDtypeStruct((own, N1, 2 * N2), F32),
        compiler_params=pltpu.CompilerParams(vmem_limit_bytes=VMEM_LIMIT),
        cost_estimate=pl.CostEstimate(flops=12 * own * N1 * N1 * 2 * N2, bytes_accessed=6 << 20, transcendentals=0),
        name="filter_spectrum",
    )(jnp.stack([half_place, first_channel]).astype(jnp.int32), skip, filters, table, twist)


PIECES = 4


def conv_kernel(
    x_ref, h_any, taps_ref, table_any, twist_any, o_any,
    grid_ref, edge_ref, res_ref, h_ref, table, twist, o_ref, h_sem, t_sem, o_sem,
):
    own = h_ref.shape[0]
    rows, width = x_ref.shape
    blocks = rows // own
    tiles = width // LANES - 1
    half = blocks // 2
    share = rows // PIECES
    cuts = [(0, 4 * N1), (4 * N1, 2 * N1), (BACK, 4 * N1), (GATHER, 2 * LANES)]
    t_copies = [
        pltpu.make_async_copy(table_any.at[pl.ds(at, n), :], table.at[pl.ds(at, n), :], t_sem.at[i])
        for i, (at, n) in enumerate(cuts)
    ]
    twist_copy = pltpu.make_async_copy(twist_any, twist, t_sem.at[len(cuts)])
    h_copies = [
        pltpu.make_async_copy(h_any.at[pl.ds(2 * i, 2)], h_ref.at[pl.ds(2 * i, 2)], h_sem.at[i]) for i in range(own // 2)
    ]
    for copy in [t_copies[3], t_copies[0], twist_copy, t_copies[1], *h_copies, t_copies[2]]:
        copy.start()

    def unpack(i, carry):
        for q in range(tiles + 1):
            tile = x_ref[rows_at(i, 2 * own), q * LANES : (q + 1) * LANES].astype(F32)
            for h in range(2):
                place = i + h * half
                if q < tiles:
                    grid_ref[rows_at(place * tiles + q, own), :] = tile[h * own : (h + 1) * own]
                else:
                    edge_ref[rows_at(place + 1, own), :] = tile[h * own : (h + 1) * own]
        return carry

    per_piece = half // PIECES
    lax.fori_loop(0, half, unpack, 0, unroll=8)

    edge_ref[:own, :] = jnp.zeros((own, LANES), F32)
    lane = lax.broadcasted_iota(jnp.int32, (rows, LANES), 1)
    both = jnp.where(lane % (LANES // 2) < EDGE, edge_ref[:rows, :], edge_ref[own:, :]).astype(BF16)
    t_copies[3].wait()
    terms = mm(both, table[GATHER : GATHER + LANES, :LANES]).reshape(blocks, own, LANES) * taps_ref[...][None]
    hi, lo = split(terms.reshape(rows, LANES))
    add = table[GATHER + LANES : GATHER + 2 * LANES]
    sums = mm(hi, add) + mm(lo, add)
    gated = sums[:, :LANES] * sums[:, LANES:]
    for p in range(blocks):
        grid_ref[p * tiles * own : (p * tiles + 1) * own, :EDGE] = gated[p * own : (p + 1) * own, :EDGE]

    pairs = range(own // 2)
    t_copies[0].wait()
    twist_copy.wait()
    twr, twi = twist[:N1], twist[N1:]
    turned = []
    for c in pairs:
        x = pair_of(grid_ref, c, own).astype(BF16)
        part = mm(table[: 2 * N1], x) + mm(table[2 * N1 : 4 * N1], x)
        for a in range(2):
            re, im = part[:N1, a * N2 : (a + 1) * N2], part[N1:, a * N2 : (a + 1) * N2]
            turned.append(jnp.concatenate([re * twr - im * twi, re * twi + im * twr], 1))
    t_copies[1].wait()
    back = []
    for c in range(own):
        if c % 2 == 0:
            h_copies[c // 2].wait()
        spec = mm3(turned[c], table[COLS_HI], table[COLS_LO])
        sr, si = spec[:, :N2], spec[:, N2:]
        hr, hi = h_ref[c, :, :N2], h_ref[c, :, N2:]
        mid = mm3(jnp.concatenate([sr * hr + si * hi, sr * hi - si * hr], 1), table[COLS_HI], table[COLS_LO])
        mr, mi = mid[:, :N2], mid[:, N2:]
        back.append((mr * twr - mi * twi, mi * twr + mr * twi))
    t_copies[2].wait()
    for c in pairs:
        y = None
        for part in range(2):
            at = BACK + part * N1
            hi, lo = split(jnp.concatenate([back[2 * c][part], back[2 * c + 1][part]], 1))
            top, low = table[at : at + N1], table[at + 2 * N1 : at + 3 * N1]
            term = mm(top, hi) + mm(top, lo) + mm(low, hi)
            y = term if y is None else y + term
        for a in range(2):
            res_ref[pl.ds(2 * c + a, N1, stride=own), :] = y[:, a * N2 : (a + 1) * N2]

    def pack(i, carry):
        for q in range(tiles):
            tile = [res_ref[rows_at((i + h * half) * tiles + q, own), :] for h in range(2)]
            o_ref[rows_at(i, 2 * own), q * LANES : (q + 1) * LANES] = jnp.concatenate(tile, 0).astype(BF16)
        return carry

    o_copies = []
    for i in range(PIECES):
        lax.fori_loop(i * per_piece, (i + 1) * per_piece, pack, 0, unroll=4)
        piece = pl.ds(i * share, share)
        o_copies.append(pltpu.make_async_copy(o_ref.at[piece, :], o_any.at[piece, :], o_sem.at[i]))
        o_copies[-1].start()
    for copy in o_copies:
        copy.wait()


def conv_call(blocks, spectrum, taps, table, twist):
    own = spectrum.shape[0]
    rows, width = blocks.shape
    out = (rows, width - LANES)
    return pl.pallas_call(
        conv_kernel,
        in_specs=[pl.BlockSpec(memory_space=pltpu.VMEM), ANY, pl.BlockSpec(memory_space=pltpu.VMEM), ANY, ANY],
        out_specs=ANY,
        out_shape=jax.ShapeDtypeStruct(out, BF16),
        scratch_shapes=[
            pltpu.VMEM((N1 * own, N2), F32),
            pltpu.VMEM((rows + own, LANES), F32),
            pltpu.VMEM((N1 * own, N2), F32),
            pltpu.VMEM(spectrum.shape, F32),
            pltpu.VMEM(table.shape, BF16),
            pltpu.VMEM(twist.shape, F32),
            pltpu.VMEM(out, BF16),
            pltpu.SemaphoreType.DMA((own // 2,)),
            pltpu.SemaphoreType.DMA((5,)),
            pltpu.SemaphoreType.DMA((PIECES,)),
        ],
        compiler_params=pltpu.CompilerParams(vmem_limit_bytes=CONV_LIMIT),
        cost_estimate=pl.CostEstimate(flops=22 * own * N1 * N1 * 2 * N2, bytes_accessed=6 << 20, transcendentals=0),
        name="long_convolution",
    )(blocks, spectrum, taps, table, twist)


def shards(features, short_taps, filters, skip):
    size = features.shape[2]
    positions = lax.axis_size("half") * lax.axis_size("ctx")
    own = filters.shape[0] // lax.axis_size("half")
    half_place, ctx_place = lax.axis_index("half"), lax.axis_index("ctx")
    first_channel = ctx_place * filters.shape[0] + half_place * own
    table, twist = transform_tables()
    taps = jnp.swapaxes(short_taps, 0, 1)

    gated = gate_call(features, taps)
    blocks = lax.all_to_all(gated, ("ctx", "half"), 0, 0, tiled=True)

    tail = features[0, :, size - EDGE :].T
    halo = lax.ppermute(tail, ("half", "ctx"), [(i, i + 1) for i in range(positions - 1)])
    spectrum = filter_call(filters, skip, half_place, first_channel, own, table, twist)
    own_taps = lax.dynamic_slice_in_dim(taps[1:], first_channel, own, 2)
    own_taps = jnp.pad(own_taps.transpose(2, 0, 1), ((0, 0), (0, 0), (0, 8 - TAPS)))
    own_taps = jnp.repeat(own_taps.reshape(own, 16), 8, axis=1)
    halo, spectrum = lax.optimization_barrier((halo, spectrum))

    convolved = conv_call(blocks, spectrum, own_taps, table, twist)
    back = lax.all_to_all(convolved, ("ctx", "half"), 0, 0, tiled=True)
    query = query_call(features, taps, halo)
    return (query * back.astype(F32)).astype(BF16)


def solution(mesh):
    in_specs = (P("seq", None, ("half", "ctx")), P(), P("ctx", None), P())
    out_specs = P("seq", ("half", "ctx"))
    return jax.shard_map(shards, mesh=mesh, in_specs=in_specs, out_specs=out_specs, check_vma=False)
```

```python
import math

import jax
import jax.numpy as jnp
import ml_dtypes
import numpy as np
from jax import lax
from jax.experimental import pallas as pl
from jax.experimental.pallas import tpu as pltpu
from jax.sharding import PartitionSpec as P

TAPS = 7
EDGE = TAPS - 1
LANES = 128
N1 = 256
N2 = 128
TOTAL = N1 * N2
F32 = jnp.float32
BF16 = jnp.bfloat16


def halves(table):
    hi = table.astype(ml_dtypes.bfloat16)
    lo = (table - hi.astype(np.float64)).astype(ml_dtypes.bfloat16)
    return hi, lo


def transform_tables():
    k1 = np.arange(N1) + 0.25
    first = np.exp(-2j * np.pi * np.outer(k1, np.arange(N1)) / N1)
    twist = np.exp(-2j * np.pi * np.outer(k1, np.arange(N2)) / TOTAL)
    second = np.exp(-2j * np.pi * np.outer(np.arange(N2), np.arange(N2)) / N2)
    rows = np.concatenate([first.real, first.imag], 0)
    columns = np.block([[second.real, second.imag], [-second.imag, second.real]])
    back = np.concatenate([first.real.T, -first.imag.T], 0)
    gather, add = np.zeros((LANES, 2 * LANES)), np.zeros((LANES, 2 * LANES))
    for branch in range(2):
        for j in range(TAPS):
            for t in range(EDGE):
                at = branch * LANES // 2 + j * 8 + t
                gather[branch * LANES // 4 + EDGE + t - j, at] = 1
                add[at, branch * LANES + t] = 1
    exact = [gather.astype(ml_dtypes.bfloat16), add.astype(ml_dtypes.bfloat16)]
    table = np.concatenate([*halves(rows), *halves(columns), *halves(back), *exact], 0)
    return jnp.asarray(table), jnp.asarray(np.concatenate([twist.real, twist.imag], 0).astype(np.float32))


ROWS = slice(0, 4 * N1)
COLS_HI, COLS_LO = slice(4 * N1, 5 * N1), slice(5 * N1, 6 * N1)
BACK = 6 * N1
GATHER = 10 * N1
FORWARD = slice(0, BACK)
VMEM_LIMIT = 60 * 1024 * 1024
CONV_LIMIT = 54525952


def mm(a, b):
    return jnp.dot(a, b, preferred_element_type=F32)


def split(x):
    hi = x.astype(BF16)
    return hi, (x - hi.astype(F32)).astype(BF16)


def mm3(x, whi, wlo):
    hi, lo = split(x)
    return mm(hi, whi) + mm(lo, whi) + mm(hi, wlo)


def rows_at(i, count):
    return pl.ds(pl.multiple_of(i * count, count), count)


GROUP = 8
PAIR = 2 * GROUP


def block_rows(tiles):
    return tiles * PAIR + GROUP


STEP = 256


def fill_selectors(shift_ref, spread_ref):
    shape = shift_ref.shape
    row, col = lax.broadcasted_iota(jnp.int32, shape, 0), lax.broadcasted_iota(jnp.int32, shape, 1)
    shift_ref[...] = jnp.where(row == LANES + col % LANES - (col // LANES + 1), 1.0, 0.0).astype(BF16)
    shape = spread_ref.shape
    row, col = lax.broadcasted_iota(jnp.int32, shape, 0), lax.broadcasted_iota(jnp.int32, shape, 1)
    spread_ref[...] = jnp.where((row < 24) & (row % 8 == col // LANES), 1.0, 0.0).astype(BF16)


def spread_taps(taps_ref, branch, start, spread):
    taps = jnp.concatenate([taps_ref[branch, :, pl.ds(start, STEP)], jnp.zeros((1, STEP), F32)], 0)
    hi = taps.astype(BF16).astype(F32)
    mid = (taps - hi).astype(BF16).astype(F32)
    columns = jnp.concatenate([hi, mid, taps - hi - mid, jnp.zeros((LANES - 24, STEP), F32)], 0).T
    return mm(columns.astype(BF16), spread)


BY_MATRIX = 4


def shaped_tile(previous, current, taps, shift):
    moved = mm(jnp.concatenate([previous, current], 1), shift[:, : BY_MATRIX * LANES])
    before, here = previous.astype(F32), current.astype(F32)
    lane = lax.broadcasted_iota(jnp.int32, here.shape, 1)
    total = taps[:, :LANES] * here
    for j in range(1, TAPS):
        if j <= BY_MATRIX:
            x = moved[:, (j - 1) * LANES : j * LANES]
        else:
            x = pltpu.roll(jnp.where(lane >= LANES - j, before, here), j, 1)
        total = total + taps[:, j * LANES : (j + 1) * LANES] * x
    return total


def gate_kernel(taps_ref, k_ref, v_ref, o_ref, shift, spread, ktaps, vtaps):
    @pl.when(pl.program_id(0) == 0)
    def _():
        fill_selectors(shift, spread)

    start = pl.multiple_of(pl.program_id(0) * STEP, STEP)
    size = k_ref.shape[2]
    tiles = size // LANES
    ktaps[...] = spread_taps(taps_ref, 1, start, spread[...])
    vtaps[...] = spread_taps(taps_ref, 2, start, spread[...])

    def tile(ref, q):
        return ref[0, :, q * LANES : (q + 1) * LANES]

    each = block_rows(tiles)
    blocks = STEP // PAIR
    for q in range(tiles):
        key = shaped_tile(tile(k_ref, (q - 1) % tiles), tile(k_ref, q), ktaps[...], shift[...])
        value = shaped_tile(tile(v_ref, (q - 1) % tiles), tile(v_ref, q), vtaps[...], shift[...])
        gated = (key * value).astype(BF16)
        for d in range(blocks):
            o_ref[d * each + q * PAIR : d * each + (q + 1) * PAIR, :] = gated[d * PAIR : (d + 1) * PAIR]
    lane = lax.broadcasted_iota(jnp.int32, (STEP, LANES), 1)

    def edges(ref, by):
        ends = jnp.where(lane >= LANES - EDGE, tile(ref, tiles - 1).astype(F32), tile(ref, 0).astype(F32))
        return pltpu.roll(ends, by, 1)

    both = jnp.where(lane < LANES // 4, edges(k_ref, EDGE), edges(v_ref, EDGE + LANES // 4))
    moved = pltpu.roll(both, LANES // 2, 1)
    lane = lax.broadcasted_iota(jnp.int32, (GROUP, LANES), 1)
    for d in range(blocks):
        at = d * PAIR
        first, second = both[at : at + GROUP], moved[at + GROUP : at + PAIR]
        o_ref[d * each + tiles * PAIR : (d + 1) * each, :] = jnp.where(lane < LANES // 2, first, second).astype(BF16)


def short_scratch(count):
    return [
        pltpu.VMEM((2 * LANES, BY_MATRIX * LANES), BF16),
        pltpu.VMEM((LANES, TAPS * LANES), BF16),
        *[pltpu.VMEM((STEP, TAPS * LANES), F32)] * count,
    ]


def gate_call(features, taps):
    _, channels, size = features.shape
    each = block_rows(size // LANES)
    return pl.pallas_call(
        gate_kernel,
        grid=(channels // STEP,),
        in_specs=[
            pl.BlockSpec(taps.shape, lambda g: (0, 0, 0)),
            pl.BlockSpec((1, STEP, size), lambda g: (1, g, 0)),
            pl.BlockSpec((1, STEP, size), lambda g: (2, g, 0)),
        ],
        out_specs=pl.BlockSpec((STEP // PAIR * each, LANES), lambda g: (g, 0)),
        out_shape=jax.ShapeDtypeStruct((channels // PAIR * each, LANES), BF16),
        scratch_shapes=short_scratch(2),
        compiler_params=pltpu.CompilerParams(vmem_limit_bytes=VMEM_LIMIT),
        cost_estimate=pl.CostEstimate(flops=60 * channels * size, bytes_accessed=6 * channels * size, transcendentals=0),
        name="gate",
    )(taps, features, features)


def query_kernel(taps_ref, halo_ref, q_ref, o_ref, shift, spread, qtaps):
    @pl.when(pl.program_id(0) == 0)
    def _():
        fill_selectors(shift, spread)

    start = pl.multiple_of(pl.program_id(0) * STEP, STEP)
    qtaps[...] = spread_taps(taps_ref, 0, start, spread[...])
    halo = halo_ref[...].astype(F32)
    previous = jnp.concatenate([jnp.zeros((LANES - EDGE, STEP), F32), halo], 0).T.astype(BF16)
    for q in range(q_ref.shape[2] // LANES):
        current = q_ref[0, :, q * LANES : (q + 1) * LANES]
        o_ref[:, q * LANES : (q + 1) * LANES] = shaped_tile(previous, current, qtaps[...], shift[...])
        previous = current


def query_call(features, taps, halo):
    _, channels, size = features.shape
    return pl.pallas_call(
        query_kernel,
        grid=(channels // STEP,),
        in_specs=[
            pl.BlockSpec(taps.shape, lambda g: (0, 0, 0)),
            pl.BlockSpec((EDGE, STEP), lambda g: (0, g)),
            pl.BlockSpec((1, STEP, size), lambda g: (0, g, 0)),
        ],
        out_specs=pl.BlockSpec((STEP, size), lambda g: (g, 0)),
        out_shape=pltpu.VMEM((channels, size), F32),
        scratch_shapes=short_scratch(1),
        cost_estimate=pl.CostEstimate(flops=30 * channels * size, bytes_accessed=6 * channels * size, transcendentals=0),
        name="query",
    )(taps, halo, features)


ANY = pl.BlockSpec(memory_space=pl.ANY)


def pair_of(grid_ref, c, own):
    return jnp.concatenate([grid_ref[pl.ds(2 * c + a, N1, stride=own), :] for a in range(2)], 1)


def filter_kernel(place_ref, skip_ref, f_ref, table_any, twist_ref, o_ref, grid_ref, table, sem):
    copy = pltpu.make_async_copy(table_any.at[FORWARD, :], table, sem)
    copy.start()
    own = f_ref.shape[0]
    for j in range(N1):
        grid_ref[j * own : (j + 1) * own, :] = f_ref[:, j * N2 : (j + 1) * N2]
    copy.wait()

    def pair(c, carry):
        hi, lo = split(pair_of(grid_ref, c, own))
        top, low = table[: 2 * N1], table[2 * N1 : 4 * N1]
        part = mm(top, hi) + mm(low, hi) + mm(top, lo)
        twr, twi = twist_ref[:N1], twist_ref[N1:]
        for a in range(2):
            re, im = part[:N1, a * N2 : (a + 1) * N2], part[N1:, a * N2 : (a + 1) * N2]
            turned = jnp.concatenate([re * twr - im * twi, re * twi + im * twr], 1)
            spec = mm3(turned, table[COLS_HI], table[COLS_LO])
            skip = skip_ref[place_ref[1] + 2 * c + a]
            o_ref[2 * c + a, :, :N2] = (spec[:, :N2] + skip) * (1.0 / TOTAL)
            o_ref[2 * c + a, :, N2:] = spec[:, N2:] * (-1.0 / TOTAL)
        return carry

    lax.fori_loop(0, own // 2, pair, 0)


def filter_call(filters, skip, half_place, first_channel, own, table, twist):
    return pl.pallas_call(
        filter_kernel,
        grid_spec=pltpu.PrefetchScalarGridSpec(
            num_scalar_prefetch=1,
            grid=(1,),
            in_specs=[
                pl.BlockSpec(memory_space=pltpu.SMEM),
                pl.BlockSpec((own, filters.shape[1]), lambda g, place: (place[0], 0)),
                ANY,
                pl.BlockSpec(twist.shape, lambda g, place: (0, 0)),
            ],
            out_specs=pl.BlockSpec((own, N1, 2 * N2), lambda g, place: (0, 0, 0)),
            scratch_shapes=[pltpu.VMEM((N1 * own, N2), F32), pltpu.VMEM((BACK, N1), BF16), pltpu.SemaphoreType.DMA],
        ),
        out_shape=jax.ShapeDtypeStruct((own, N1, 2 * N2), F32),
        compiler_params=pltpu.CompilerParams(vmem_limit_bytes=VMEM_LIMIT),
        cost_estimate=pl.CostEstimate(flops=12 * own * N1 * N1 * 2 * N2, bytes_accessed=6 << 20, transcendentals=0),
        name="filter_spectrum",
    )(jnp.stack([half_place, first_channel]).astype(jnp.int32), skip, filters, table, twist)


PIECES = 4


def conv_kernel(
    half_ref, own_ref, other_ref, h_any, taps_ref, table_any, twist_any, o_any,
    grid_ref, edge_ref, res_ref, h_ref, table, twist, o_ref, h_sem, t_sem, o_sem,
):
    own = h_ref.shape[0]
    rows, size = o_ref.shape
    blocks = rows // own
    tiles = size // LANES
    half = blocks // 2
    share = rows // PIECES
    per_piece = half // PIECES
    cuts = [(0, 4 * N1), (4 * N1, 2 * N1), (BACK, 4 * N1), (GATHER, 2 * LANES)]
    t_copies = [
        pltpu.make_async_copy(table_any.at[pl.ds(at, n), :], table.at[pl.ds(at, n), :], t_sem.at[i])
        for i, (at, n) in enumerate(cuts)
    ]
    twist_copy = pltpu.make_async_copy(twist_any, twist, t_sem.at[len(cuts)])
    h_copies = [
        pltpu.make_async_copy(h_any.at[pl.ds(2 * i, 2)], h_ref.at[pl.ds(2 * i, 2)], h_sem.at[i]) for i in range(own // 2)
    ]
    for copy in [t_copies[3], t_copies[0], twist_copy, t_copies[1], *h_copies, t_copies[2]]:
        copy.start()

    place = half_ref[0]
    each = block_rows(tiles)
    for ref, side in ((own_ref, place), (other_ref, 1 - place)):
        for i in range(half):
            to = i + side * half
            for q in range(tiles):
                tile = ref[i * each + q * PAIR : i * each + (q + 1) * PAIR, :].astype(F32)
                grid_ref[rows_at(to * tiles + q, own), :] = jnp.where(place == 0, tile[:own], tile[own:])
            edge = ref[i * each + tiles * PAIR : (i + 1) * each, :].astype(F32)
            edge_ref[rows_at(to + 1, own), :] = jnp.where(place == 0, edge, pltpu.roll(edge, LANES // 2, 1))

    edge_ref[:own, :] = jnp.zeros((own, LANES), F32)
    lane = lax.broadcasted_iota(jnp.int32, (rows, LANES), 1)
    both = jnp.where(lane % (LANES // 4) < EDGE, edge_ref[:rows, :], edge_ref[own:, :]).astype(BF16)
    t_copies[3].wait()
    terms = mm(both, table[GATHER : GATHER + LANES, :LANES]).reshape(blocks, own, LANES) * taps_ref[...][None]
    hi, lo = split(terms.reshape(rows, LANES))
    add = table[GATHER + LANES : GATHER + 2 * LANES]
    sums = mm(hi, add) + mm(lo, add)
    gated = sums[:, :LANES] * sums[:, LANES:]
    for p in range(blocks):
        grid_ref[p * tiles * own : (p * tiles + 1) * own, :EDGE] = gated[p * own : (p + 1) * own, :EDGE]

    pairs = range(own // 2)
    t_copies[0].wait()
    twist_copy.wait()
    twr, twi = twist[:N1], twist[N1:]
    turned = []
    for c in pairs:
        x = pair_of(grid_ref, c, own).astype(BF16)
        part = mm(table[: 2 * N1], x) + mm(table[2 * N1 : 4 * N1], x)
        for a in range(2):
            re, im = part[:N1, a * N2 : (a + 1) * N2], part[N1:, a * N2 : (a + 1) * N2]
            turned.append(jnp.concatenate([re * twr - im * twi, re * twi + im * twr], 1))
    t_copies[1].wait()
    back = []
    for c in range(own):
        if c % 2 == 0:
            h_copies[c // 2].wait()
        spec = mm3(turned[c], table[COLS_HI], table[COLS_LO])
        sr, si = spec[:, :N2], spec[:, N2:]
        hr, hi = h_ref[c, :, :N2], h_ref[c, :, N2:]
        mid = mm3(jnp.concatenate([sr * hr + si * hi, sr * hi - si * hr], 1), table[COLS_HI], table[COLS_LO])
        mr, mi = mid[:, :N2], mid[:, N2:]
        back.append((mr * twr - mi * twi, mi * twr + mr * twi))
    t_copies[2].wait()
    for c in pairs:
        y = None
        for part in range(2):
            at = BACK + part * N1
            hi, lo = split(jnp.concatenate([back[2 * c][part], back[2 * c + 1][part]], 1))
            top, low = table[at : at + N1], table[at + 2 * N1 : at + 3 * N1]
            term = mm(top, hi) + mm(top, lo) + mm(low, hi)
            y = term if y is None else y + term
        for a in range(2):
            res_ref[pl.ds(2 * c + a, N1, stride=own), :] = y[:, a * N2 : (a + 1) * N2]

    o_copies = []
    for i in range(PIECES):
        for g in range(i * per_piece, (i + 1) * per_piece):
            for q in range(tiles):
                at = [((g + h * half) * tiles + q) * own for h in range(2)]
                tile = jnp.concatenate([res_ref[a : a + own, :] for a in at], 0)
                o_ref[g * 2 * own : (g + 1) * 2 * own, q * LANES : (q + 1) * LANES] = tile.astype(BF16)
        piece = pl.ds(i * share, share)
        o_copies.append(pltpu.make_async_copy(o_ref.at[piece, :], o_any.at[piece, :], o_sem.at[i]))
        o_copies[-1].start()
    for copy in o_copies:
        copy.wait()


def conv_call(half_place, blocks, others, spectrum, taps, table, twist, out):
    own = spectrum.shape[0]
    rows = out[0]
    vmem = pl.BlockSpec(memory_space=pltpu.VMEM)
    return pl.pallas_call(
        conv_kernel,
        in_specs=[pl.BlockSpec(memory_space=pltpu.SMEM), vmem, vmem, ANY, vmem, ANY, ANY],
        out_specs=ANY,
        out_shape=jax.ShapeDtypeStruct(out, BF16),
        scratch_shapes=[
            pltpu.VMEM((N1 * own, N2), F32),
            pltpu.VMEM((rows + own, LANES), F32),
            pltpu.VMEM((N1 * own, N2), F32),
            pltpu.VMEM(spectrum.shape, F32),
            pltpu.VMEM(table.shape, BF16),
            pltpu.VMEM(twist.shape, F32),
            pltpu.VMEM(out, BF16),
            pltpu.SemaphoreType.DMA((own // 2,)),
            pltpu.SemaphoreType.DMA((5,)),
            pltpu.SemaphoreType.DMA((PIECES,)),
        ],
        compiler_params=pltpu.CompilerParams(vmem_limit_bytes=CONV_LIMIT),
        cost_estimate=pl.CostEstimate(flops=22 * own * N1 * N1 * 2 * N2, bytes_accessed=6 << 20, transcendentals=0),
        name="long_convolution",
    )(half_place.reshape(1).astype(jnp.int32), blocks, others, spectrum, taps, table, twist)


def shards(features, short_taps, filters, skip):
    size = features.shape[2]
    positions = lax.axis_size("half") * lax.axis_size("ctx")
    own = filters.shape[0] // lax.axis_size("half")
    half_place, ctx_place = lax.axis_index("half"), lax.axis_index("ctx")
    first_channel = ctx_place * filters.shape[0] + half_place * own
    table, twist = transform_tables()
    taps = jnp.swapaxes(short_taps, 0, 1)

    gated = gate_call(features, taps)
    blocks = lax.all_to_all(gated, "ctx", 0, 0, tiled=True)

    tail = features[0, :, size - EDGE :].T
    halo = lax.ppermute(tail, ("half", "ctx"), [(i, i + 1) for i in range(positions - 1)])
    spectrum = filter_call(filters, skip, half_place, first_channel, own, table, twist)
    own_taps = lax.dynamic_slice_in_dim(taps[1:], first_channel, own, 2)
    own_taps = jnp.pad(own_taps.transpose(2, 0, 1), ((0, 0), (0, 0), (0, 8 - TAPS)))
    own_taps = jnp.repeat(own_taps.reshape(own, 16), 8, axis=1)
    blocks, halo, spectrum, own_taps = lax.optimization_barrier((blocks, halo, spectrum, own_taps))
    others = lax.ppermute(blocks, "half", [(0, 1), (1, 0)])

    out = (positions * own, size)
    convolved = conv_call(half_place, blocks, others, spectrum, own_taps, table, twist, out)
    back = lax.all_to_all(convolved, ("ctx", "half"), 0, 0, tiled=True)
    query = query_call(features, taps, halo)
    return (query * back.astype(F32)).astype(BF16)


def solution(mesh):
    in_specs = (P("seq", None, ("half", "ctx")), P(), P("ctx", None), P())
    out_specs = P("seq", ("half", "ctx"))
    return jax.shard_map(shards, mesh=mesh, in_specs=in_specs, out_specs=out_specs, check_vma=False)
```

```python
import math

import jax
import jax.numpy as jnp
import ml_dtypes
import numpy as np
from jax import lax
from jax.experimental import pallas as pl
from jax.experimental.pallas import tpu as pltpu
from jax.sharding import PartitionSpec as P

TAPS = 7
EDGE = TAPS - 1
LANES = 128
N1 = 256
N2 = 128
TOTAL = N1 * N2
F32 = jnp.float32
BF16 = jnp.bfloat16


def halves(table):
    hi = table.astype(ml_dtypes.bfloat16)
    lo = (table - hi.astype(np.float64)).astype(ml_dtypes.bfloat16)
    return hi, lo


def transform_tables():
    k1 = np.arange(N1) + 0.25
    first = np.exp(-2j * np.pi * np.outer(k1, np.arange(N1)) / N1)
    twist = np.exp(-2j * np.pi * np.outer(k1, np.arange(N2)) / TOTAL)
    second = np.exp(-2j * np.pi * np.outer(np.arange(N2), np.arange(N2)) / N2)
    rows = np.concatenate([first.real, first.imag], 0)
    columns = np.block([[second.real, second.imag], [-second.imag, second.real]])
    back = np.concatenate([first.real.T, -first.imag.T], 0)
    gather, add = np.zeros((LANES, 2 * LANES)), np.zeros((LANES, 2 * LANES))
    for branch in range(2):
        for j in range(TAPS):
            for t in range(EDGE):
                at = branch * LANES // 2 + j * 8 + t
                gather[branch * LANES // 4 + EDGE + t - j, at] = 1
                add[at, branch * LANES + t] = 1
    exact = [gather.astype(ml_dtypes.bfloat16), add.astype(ml_dtypes.bfloat16)]
    table = np.concatenate([*halves(rows), *halves(columns), *halves(back), *exact], 0)
    return jnp.asarray(table), jnp.asarray(np.concatenate([twist.real, twist.imag], 0).astype(np.float32))


ROWS = slice(0, 4 * N1)
COLS_HI, COLS_LO = slice(4 * N1, 5 * N1), slice(5 * N1, 6 * N1)
BACK = 6 * N1
GATHER = 10 * N1
FORWARD = slice(0, BACK)
VMEM_LIMIT = 60 * 1024 * 1024
CONV_LIMIT = 52428800


def mm(a, b):
    return jnp.dot(a, b, preferred_element_type=F32)


def split(x):
    hi = x.astype(BF16)
    return hi, (x - hi.astype(F32)).astype(BF16)


def mm3(x, whi, wlo):
    hi, lo = split(x)
    return mm(hi, whi) + mm(lo, whi) + mm(hi, wlo)


def rows_at(i, count):
    return pl.ds(pl.multiple_of(i * count, count), count)


GROUP = 8
PAIR = 2 * GROUP


def block_rows(tiles):
    return tiles * PAIR + GROUP


STEP = 256


def fill_selectors(shift_ref, spread_ref):
    shape = shift_ref.shape
    row, col = lax.broadcasted_iota(jnp.int32, shape, 0), lax.broadcasted_iota(jnp.int32, shape, 1)
    shift_ref[...] = jnp.where(row == LANES + col % LANES - (col // LANES + 1), 1.0, 0.0).astype(BF16)
    shape = spread_ref.shape
    row, col = lax.broadcasted_iota(jnp.int32, shape, 0), lax.broadcasted_iota(jnp.int32, shape, 1)
    spread_ref[...] = jnp.where((row < 24) & (row % 8 == col // LANES), 1.0, 0.0).astype(BF16)


def spread_taps(taps_ref, branch, start, spread):
    taps = jnp.concatenate([taps_ref[branch, :, pl.ds(start, STEP)], jnp.zeros((1, STEP), F32)], 0)
    hi = taps.astype(BF16).astype(F32)
    mid = (taps - hi).astype(BF16).astype(F32)
    columns = jnp.concatenate([hi, mid, taps - hi - mid, jnp.zeros((LANES - 24, STEP), F32)], 0).T
    return mm(columns.astype(BF16), spread)


BY_MATRIX = 4


def shaped_tile(previous, current, taps, shift):
    moved = mm(jnp.concatenate([previous, current], 1), shift[:, : BY_MATRIX * LANES])
    before, here = previous.astype(F32), current.astype(F32)
    lane = lax.broadcasted_iota(jnp.int32, here.shape, 1)
    total = taps[:, :LANES] * here
    for j in range(1, TAPS):
        if j <= BY_MATRIX:
            x = moved[:, (j - 1) * LANES : j * LANES]
        else:
            x = pltpu.roll(jnp.where(lane >= LANES - j, before, here), j, 1)
        total = total + taps[:, j * LANES : (j + 1) * LANES] * x
    return total


def gate_kernel(taps_ref, k_ref, v_ref, o_ref, shift, spread, ktaps, vtaps):
    @pl.when(pl.program_id(0) == 0)
    def _():
        fill_selectors(shift, spread)

    start = pl.multiple_of(pl.program_id(0) * STEP, STEP)
    size = k_ref.shape[2]
    tiles = size // LANES
    ktaps[...] = spread_taps(taps_ref, 1, start, spread[...])
    vtaps[...] = spread_taps(taps_ref, 2, start, spread[...])

    def tile(ref, q):
        return ref[0, :, q * LANES : (q + 1) * LANES]

    each = block_rows(tiles)
    blocks = STEP // PAIR
    for q in range(tiles):
        key = shaped_tile(tile(k_ref, (q - 1) % tiles), tile(k_ref, q), ktaps[...], shift[...])
        value = shaped_tile(tile(v_ref, (q - 1) % tiles), tile(v_ref, q), vtaps[...], shift[...])
        gated = (key * value).astype(BF16)
        for d in range(blocks):
            o_ref[d * each + q * PAIR : d * each + (q + 1) * PAIR, :] = gated[d * PAIR : (d + 1) * PAIR]
    lane = lax.broadcasted_iota(jnp.int32, (STEP, LANES), 1)

    def edges(ref, by):
        ends = jnp.where(lane >= LANES - EDGE, tile(ref, tiles - 1).astype(F32), tile(ref, 0).astype(F32))
        return pltpu.roll(ends, by, 1)

    both = jnp.where(lane < LANES // 4, edges(k_ref, EDGE), edges(v_ref, EDGE + LANES // 4))
    moved = pltpu.roll(both, LANES // 2, 1)
    lane = lax.broadcasted_iota(jnp.int32, (GROUP, LANES), 1)
    for d in range(blocks):
        at = d * PAIR
        first, second = both[at : at + GROUP], moved[at + GROUP : at + PAIR]
        o_ref[d * each + tiles * PAIR : (d + 1) * each, :] = jnp.where(lane < LANES // 2, first, second).astype(BF16)


def short_scratch(count):
    return [
        pltpu.VMEM((2 * LANES, BY_MATRIX * LANES), BF16),
        pltpu.VMEM((LANES, TAPS * LANES), BF16),
        *[pltpu.VMEM((STEP, TAPS * LANES), F32)] * count,
    ]


def gate_call(features, taps):
    _, channels, size = features.shape
    each = block_rows(size // LANES)
    return pl.pallas_call(
        gate_kernel,
        grid=(channels // STEP,),
        in_specs=[
            pl.BlockSpec(taps.shape, lambda g: (0, 0, 0)),
            pl.BlockSpec((1, STEP, size), lambda g: (1, g, 0)),
            pl.BlockSpec((1, STEP, size), lambda g: (2, g, 0)),
        ],
        out_specs=pl.BlockSpec((STEP // PAIR * each, LANES), lambda g: (g, 0)),
        out_shape=jax.ShapeDtypeStruct((channels // PAIR * each, LANES), BF16),
        scratch_shapes=short_scratch(2),
        compiler_params=pltpu.CompilerParams(vmem_limit_bytes=VMEM_LIMIT),
        cost_estimate=pl.CostEstimate(flops=60 * channels * size, bytes_accessed=6 * channels * size, transcendentals=0),
        name="gate",
    )(taps, features, features)


def query_kernel(taps_ref, halo_ref, q_ref, o_ref, shift, spread, qtaps):
    @pl.when(pl.program_id(0) == 0)
    def _():
        fill_selectors(shift, spread)

    start = pl.multiple_of(pl.program_id(0) * STEP, STEP)
    qtaps[...] = spread_taps(taps_ref, 0, start, spread[...])
    halo = halo_ref[...].astype(F32)
    previous = jnp.concatenate([jnp.zeros((LANES - EDGE, STEP), F32), halo], 0).T.astype(BF16)
    for q in range(q_ref.shape[2] // LANES):
        current = q_ref[0, :, q * LANES : (q + 1) * LANES]
        o_ref[:, q * LANES : (q + 1) * LANES] = shaped_tile(previous, current, qtaps[...], shift[...])
        previous = current


def query_call(features, taps, halo):
    _, channels, size = features.shape
    return pl.pallas_call(
        query_kernel,
        grid=(channels // STEP,),
        in_specs=[
            pl.BlockSpec(taps.shape, lambda g: (0, 0, 0)),
            pl.BlockSpec((EDGE, STEP), lambda g: (0, g)),
            pl.BlockSpec((1, STEP, size), lambda g: (0, g, 0)),
        ],
        out_specs=pl.BlockSpec((STEP, size), lambda g: (g, 0)),
        out_shape=pltpu.VMEM((channels, size), F32),
        scratch_shapes=short_scratch(1),
        cost_estimate=pl.CostEstimate(flops=30 * channels * size, bytes_accessed=6 * channels * size, transcendentals=0),
        name="query",
    )(taps, halo, features)


ANY = pl.BlockSpec(memory_space=pl.ANY)


def pair_of(grid_ref, c, own):
    return jnp.concatenate([grid_ref[pl.ds(2 * c + a, N1, stride=own), :] for a in range(2)], 1)


def filter_kernel(place_ref, skip_ref, f_ref, table_any, twist_ref, o_ref, grid_ref, table, sem):
    copy = pltpu.make_async_copy(table_any.at[FORWARD, :], table, sem)
    copy.start()
    own = f_ref.shape[0]
    for j in range(N1):
        grid_ref[j * own : (j + 1) * own, :] = f_ref[:, j * N2 : (j + 1) * N2]
    copy.wait()

    def pair(c, carry):
        hi, lo = split(pair_of(grid_ref, c, own))
        top, low = table[: 2 * N1], table[2 * N1 : 4 * N1]
        part = mm(top, hi) + mm(low, hi) + mm(top, lo)
        twr, twi = twist_ref[:N1], twist_ref[N1:]
        for a in range(2):
            re, im = part[:N1, a * N2 : (a + 1) * N2], part[N1:, a * N2 : (a + 1) * N2]
            turned = jnp.concatenate([re * twr - im * twi, re * twi + im * twr], 1)
            spec = mm3(turned, table[COLS_HI], table[COLS_LO])
            skip = skip_ref[place_ref[1] + 2 * c + a]
            o_ref[2 * c + a, :, :N2] = (spec[:, :N2] + skip) * (1.0 / TOTAL)
            o_ref[2 * c + a, :, N2:] = spec[:, N2:] * (-1.0 / TOTAL)
        return carry

    lax.fori_loop(0, own // 2, pair, 0)


def filter_call(filters, skip, half_place, first_channel, own, table, twist):
    return pl.pallas_call(
        filter_kernel,
        grid_spec=pltpu.PrefetchScalarGridSpec(
            num_scalar_prefetch=1,
            grid=(1,),
            in_specs=[
                pl.BlockSpec(memory_space=pltpu.SMEM),
                pl.BlockSpec((own, filters.shape[1]), lambda g, place: (place[0], 0)),
                ANY,
                pl.BlockSpec(twist.shape, lambda g, place: (0, 0)),
            ],
            out_specs=pl.BlockSpec((own, N1, 2 * N2), lambda g, place: (0, 0, 0)),
            scratch_shapes=[pltpu.VMEM((N1 * own, N2), F32), pltpu.VMEM((BACK, N1), BF16), pltpu.SemaphoreType.DMA],
        ),
        out_shape=jax.ShapeDtypeStruct((own, N1, 2 * N2), F32),
        compiler_params=pltpu.CompilerParams(vmem_limit_bytes=VMEM_LIMIT),
        cost_estimate=pl.CostEstimate(flops=12 * own * N1 * N1 * 2 * N2, bytes_accessed=6 << 20, transcendentals=0),
        name="filter_spectrum",
    )(jnp.stack([half_place, first_channel]).astype(jnp.int32), skip, filters, table, twist)


PIECES = 4


def conv_kernel(
    half_ref, own_ref, other_ref, h_any, taps_ref, table, twist, o_any,
    grid_ref, edge_ref, res_ref, h_ref, o_ref, h_sem, o_sem,
):
    own = h_ref.shape[0]
    rows, size = o_ref.shape
    blocks = rows // own
    tiles = size // LANES
    half = blocks // 2
    share = rows // PIECES
    per_piece = half // PIECES
    h_copy = pltpu.make_async_copy(h_any, h_ref, h_sem)
    h_copy.start()

    place = half_ref[0]
    each = block_rows(tiles)
    for ref, side in ((own_ref, place), (other_ref, 1 - place)):
        for i in range(half):
            to = i + side * half
            for q in range(tiles):
                tile = ref[i * each + q * PAIR : i * each + (q + 1) * PAIR, :].astype(F32)
                grid_ref[rows_at(to * tiles + q, own), :] = jnp.where(place == 0, tile[:own], tile[own:])
            edge = ref[i * each + tiles * PAIR : (i + 1) * each, :].astype(F32)
            edge_ref[rows_at(to + 1, own), :] = jnp.where(place == 0, edge, pltpu.roll(edge, LANES // 2, 1))

    edge_ref[:own, :] = jnp.zeros((own, LANES), F32)
    lane = lax.broadcasted_iota(jnp.int32, (rows, LANES), 1)
    both = jnp.where(lane % (LANES // 4) < EDGE, edge_ref[:rows, :], edge_ref[own:, :]).astype(BF16)
    terms = mm(both, table[GATHER : GATHER + LANES, :LANES]).reshape(blocks, own, LANES) * taps_ref[...][None]
    hi, lo = split(terms.reshape(rows, LANES))
    add = table[GATHER + LANES : GATHER + 2 * LANES]
    sums = mm(hi, add) + mm(lo, add)
    gated = sums[:, :LANES] * sums[:, LANES:]
    for p in range(blocks):
        grid_ref[p * tiles * own : (p * tiles + 1) * own, :EDGE] = gated[p * own : (p + 1) * own, :EDGE]

    pairs = range(own // 2)
    twr, twi = twist[:N1], twist[N1:]
    turned = []
    for c in pairs:
        x = pair_of(grid_ref, c, own).astype(BF16)
        part = mm(table[: 2 * N1], x) + mm(table[2 * N1 : 4 * N1], x)
        for a in range(2):
            re, im = part[:N1, a * N2 : (a + 1) * N2], part[N1:, a * N2 : (a + 1) * N2]
            turned.append(jnp.concatenate([re * twr - im * twi, re * twi + im * twr], 1))
    h_copy.wait()
    back = []
    for c in range(own):
        spec = mm3(turned[c], table[COLS_HI], table[COLS_LO])
        sr, si = spec[:, :N2], spec[:, N2:]
        hr, hi = h_ref[c, :, :N2], h_ref[c, :, N2:]
        mid = mm3(jnp.concatenate([sr * hr + si * hi, sr * hi - si * hr], 1), table[COLS_HI], table[COLS_LO])
        mr, mi = mid[:, :N2], mid[:, N2:]
        back.append((mr * twr - mi * twi, mi * twr + mr * twi))
    for c in pairs:
        y = None
        for part in range(2):
            at = BACK + part * N1
            hi, lo = split(jnp.concatenate([back[2 * c][part], back[2 * c + 1][part]], 1))
            top, low = table[at : at + N1], table[at + 2 * N1 : at + 3 * N1]
            term = mm(top, hi) + mm(top, lo) + mm(low, hi)
            y = term if y is None else y + term
        for a in range(2):
            res_ref[pl.ds(2 * c + a, N1, stride=own), :] = y[:, a * N2 : (a + 1) * N2]

    o_copies = []
    for i in range(PIECES):
        for g in range(i * per_piece, (i + 1) * per_piece):
            for q in range(tiles):
                at = [((g + h * half) * tiles + q) * own for h in range(2)]
                tile = jnp.concatenate([res_ref[a : a + own, :] for a in at], 0)
                o_ref[g * 2 * own : (g + 1) * 2 * own, q * LANES : (q + 1) * LANES] = tile.astype(BF16)
        piece = pl.ds(i * share, share)
        o_copies.append(pltpu.make_async_copy(o_ref.at[piece, :], o_any.at[piece, :], o_sem.at[i]))
        o_copies[-1].start()
    for copy in o_copies:
        copy.wait()


def conv_call(half_place, blocks, others, spectrum, taps, table, twist, out):
    own = spectrum.shape[0]
    rows = out[0]
    vmem = pl.BlockSpec(memory_space=pltpu.VMEM)
    return pl.pallas_call(
        conv_kernel,
        in_specs=[pl.BlockSpec(memory_space=pltpu.SMEM), vmem, vmem, ANY, vmem, vmem, vmem],
        out_specs=ANY,
        out_shape=jax.ShapeDtypeStruct(out, BF16),
        scratch_shapes=[
            pltpu.VMEM((N1 * own, N2), F32),
            pltpu.VMEM((rows + own, LANES), F32),
            pltpu.VMEM((N1 * own, N2), F32),
            pltpu.VMEM(spectrum.shape, F32),
            pltpu.VMEM(out, BF16),
            pltpu.SemaphoreType.DMA,
            pltpu.SemaphoreType.DMA((PIECES,)),
        ],
        compiler_params=pltpu.CompilerParams(vmem_limit_bytes=CONV_LIMIT),
        cost_estimate=pl.CostEstimate(flops=22 * own * N1 * N1 * 2 * N2, bytes_accessed=6 << 20, transcendentals=0),
        name="long_convolution",
    )(half_place.reshape(1).astype(jnp.int32), blocks, others, spectrum, taps, table, twist)


def shards(features, short_taps, filters, skip):
    size = features.shape[2]
    positions = lax.axis_size("half") * lax.axis_size("ctx")
    own = filters.shape[0] // lax.axis_size("half")
    half_place, ctx_place = lax.axis_index("half"), lax.axis_index("ctx")
    first_channel = ctx_place * filters.shape[0] + half_place * own
    table, twist = transform_tables()
    taps = jnp.swapaxes(short_taps, 0, 1)

    gated = gate_call(features, taps)
    blocks = lax.all_to_all(gated, "ctx", 0, 0, tiled=True)

    tail = features[0, :, size - EDGE :].T
    halo = lax.ppermute(tail, ("half", "ctx"), [(i, i + 1) for i in range(positions - 1)])
    spectrum = filter_call(filters, skip, half_place, first_channel, own, table, twist)
    own_taps = lax.dynamic_slice_in_dim(taps[1:], first_channel, own, 2)
    own_taps = jnp.pad(own_taps.transpose(2, 0, 1), ((0, 0), (0, 0), (0, 8 - TAPS)))
    own_taps = jnp.repeat(own_taps.reshape(own, 16), 8, axis=1)
    blocks, halo, spectrum, own_taps = lax.optimization_barrier((blocks, halo, spectrum, own_taps))
    others = lax.ppermute(blocks, "half", [(0, 1), (1, 0)])

    out = (positions * own, size)
    convolved = conv_call(half_place, blocks, others, spectrum, own_taps, table, twist, out)
    back = lax.all_to_all(convolved, ("ctx", "half"), 0, 0, tiled=True)
    query = query_call(features, taps, halo)
    return (query * back.astype(F32)).astype(BF16)


def solution(mesh):
    in_specs = (P("seq", None, ("half", "ctx")), P(), P("ctx", None), P())
    out_specs = P("seq", ("half", "ctx"))
    return jax.shard_map(shards, mesh=mesh, in_specs=in_specs, out_specs=out_specs, check_vma=False)
```

```python
import math

import jax
import jax.numpy as jnp
import ml_dtypes
import numpy as np
from jax import lax
from jax.experimental import pallas as pl
from jax.experimental.pallas import tpu as pltpu
from jax.sharding import PartitionSpec as P

TAPS = 7
EDGE = TAPS - 1
LANES = 128
N1 = 256
N2 = 128
TOTAL = N1 * N2
F32 = jnp.float32
BF16 = jnp.bfloat16


def halves(table):
    hi = table.astype(ml_dtypes.bfloat16)
    lo = (table - hi.astype(np.float64)).astype(ml_dtypes.bfloat16)
    return hi, lo


def transform_tables():
    k1 = np.arange(N1) + 0.25
    first = np.exp(-2j * np.pi * np.outer(k1, np.arange(N1)) / N1)
    twist = np.exp(-2j * np.pi * np.outer(k1, np.arange(N2)) / TOTAL)
    second = np.exp(-2j * np.pi * np.outer(np.arange(N2), np.arange(N2)) / N2)
    rows = np.concatenate([first.real, first.imag], 0)
    columns = np.block([[second.real, second.imag], [-second.imag, second.real]])
    back = np.concatenate([first.real.T, -first.imag.T], 0)
    gather, add = np.zeros((LANES, 2 * LANES)), np.zeros((LANES, 2 * LANES))
    for branch in range(2):
        for j in range(TAPS):
            for t in range(EDGE):
                at = branch * LANES // 2 + j * 8 + t
                gather[branch * LANES // 4 + EDGE + t - j, at] = 1
                add[at, branch * LANES + t] = 1
    exact = [gather.astype(ml_dtypes.bfloat16), add.astype(ml_dtypes.bfloat16)]
    table = np.concatenate([*halves(rows), *halves(columns), *halves(back), *exact], 0)
    return jnp.asarray(table), jnp.asarray(np.concatenate([twist.real, twist.imag], 0).astype(np.float32))


ROWS = slice(0, 4 * N1)
COLS_HI, COLS_LO = slice(4 * N1, 5 * N1), slice(5 * N1, 6 * N1)
BACK = 6 * N1
GATHER = 10 * N1
FORWARD = slice(0, BACK)
VMEM_LIMIT = 60 * 1024 * 1024
CONV_LIMIT = 52428800


def mm(a, b):
    return jnp.dot(a, b, preferred_element_type=F32)


def split(x):
    hi = x.astype(BF16)
    return hi, (x - hi.astype(F32)).astype(BF16)


def mm3(x, whi, wlo):
    hi, lo = split(x)
    return mm(hi, whi) + mm(lo, whi) + mm(hi, wlo)


def rows_at(i, count):
    return pl.ds(pl.multiple_of(i * count, count), count)


GROUP = 8
PAIR = 2 * GROUP


def block_rows(tiles):
    return tiles * PAIR + GROUP


STEP = 256


def fill_selectors(shift_ref, spread_ref):
    shape = shift_ref.shape
    row, col = lax.broadcasted_iota(jnp.int32, shape, 0), lax.broadcasted_iota(jnp.int32, shape, 1)
    shift_ref[...] = jnp.where(row == LANES + col % LANES - (col // LANES + 1), 1.0, 0.0).astype(BF16)
    shape = spread_ref.shape
    row, col = lax.broadcasted_iota(jnp.int32, shape, 0), lax.broadcasted_iota(jnp.int32, shape, 1)
    spread_ref[...] = jnp.where((row < 24) & (row % 8 == col // LANES), 1.0, 0.0).astype(BF16)


def spread_taps(taps_ref, branch, start, spread):
    taps = jnp.concatenate([taps_ref[branch, :, pl.ds(start, STEP)], jnp.zeros((1, STEP), F32)], 0)
    hi = taps.astype(BF16).astype(F32)
    mid = (taps - hi).astype(BF16).astype(F32)
    columns = jnp.concatenate([hi, mid, taps - hi - mid, jnp.zeros((LANES - 24, STEP), F32)], 0).T
    return mm(columns.astype(BF16), spread)


BY_MATRIX = 4


def shaped_tile(previous, current, taps, shift):
    moved = mm(jnp.concatenate([previous, current], 1), shift[:, : BY_MATRIX * LANES])
    before, here = previous.astype(F32), current.astype(F32)
    lane = lax.broadcasted_iota(jnp.int32, here.shape, 1)
    total = taps[:, :LANES] * here
    for j in range(1, TAPS):
        if j <= BY_MATRIX:
            x = moved[:, (j - 1) * LANES : j * LANES]
        else:
            x = pltpu.roll(jnp.where(lane >= LANES - j, before, here), j, 1)
        total = total + taps[:, j * LANES : (j + 1) * LANES] * x
    return total


def gate_kernel(taps_ref, k_ref, v_ref, o_ref, shift, spread, ktaps, vtaps):
    @pl.when(pl.program_id(0) == 0)
    def _():
        fill_selectors(shift, spread)

    start = pl.multiple_of(pl.program_id(0) * STEP, STEP)
    size = k_ref.shape[2]
    tiles = size // LANES
    ktaps[...] = spread_taps(taps_ref, 1, start, spread[...])
    vtaps[...] = spread_taps(taps_ref, 2, start, spread[...])

    def tile(ref, q):
        return ref[0, :, q * LANES : (q + 1) * LANES]

    each = block_rows(tiles)
    blocks = STEP // PAIR
    for q in range(tiles):
        key = shaped_tile(tile(k_ref, (q - 1) % tiles), tile(k_ref, q), ktaps[...], shift[...])
        value = shaped_tile(tile(v_ref, (q - 1) % tiles), tile(v_ref, q), vtaps[...], shift[...])
        gated = (key * value).astype(BF16)
        for d in range(blocks):
            o_ref[d * each + q * PAIR : d * each + (q + 1) * PAIR, :] = gated[d * PAIR : (d + 1) * PAIR]
    lane = lax.broadcasted_iota(jnp.int32, (STEP, LANES), 1)

    def edges(ref, by):
        ends = jnp.where(lane >= LANES - EDGE, tile(ref, tiles - 1).astype(F32), tile(ref, 0).astype(F32))
        return pltpu.roll(ends, by, 1)

    both = jnp.where(lane < LANES // 4, edges(k_ref, EDGE), edges(v_ref, EDGE + LANES // 4))
    moved = pltpu.roll(both, LANES // 2, 1)
    lane = lax.broadcasted_iota(jnp.int32, (GROUP, LANES), 1)
    for d in range(blocks):
        at = d * PAIR
        first, second = both[at : at + GROUP], moved[at + GROUP : at + PAIR]
        o_ref[d * each + tiles * PAIR : (d + 1) * each, :] = jnp.where(lane < LANES // 2, first, second).astype(BF16)


def short_scratch(count):
    return [
        pltpu.VMEM((2 * LANES, BY_MATRIX * LANES), BF16),
        pltpu.VMEM((LANES, TAPS * LANES), BF16),
        *[pltpu.VMEM((STEP, TAPS * LANES), F32)] * count,
    ]


def gate_call(features, taps):
    _, channels, size = features.shape
    each = block_rows(size // LANES)
    return pl.pallas_call(
        gate_kernel,
        grid=(channels // STEP,),
        in_specs=[
            pl.BlockSpec(taps.shape, lambda g: (0, 0, 0)),
            pl.BlockSpec((1, STEP, size), lambda g: (1, g, 0)),
            pl.BlockSpec((1, STEP, size), lambda g: (2, g, 0)),
        ],
        out_specs=pl.BlockSpec((STEP // PAIR * each, LANES), lambda g: (g, 0)),
        out_shape=jax.ShapeDtypeStruct((channels // PAIR * each, LANES), BF16),
        scratch_shapes=short_scratch(2),
        compiler_params=pltpu.CompilerParams(vmem_limit_bytes=VMEM_LIMIT),
        cost_estimate=pl.CostEstimate(flops=60 * channels * size, bytes_accessed=6 * channels * size, transcendentals=0),
        name="gate",
    )(taps, features, features)


def query_kernel(taps_ref, halo_ref, q_ref, o_ref, shift, spread, qtaps):
    @pl.when(pl.program_id(0) == 0)
    def _():
        fill_selectors(shift, spread)

    start = pl.multiple_of(pl.program_id(0) * STEP, STEP)
    qtaps[...] = spread_taps(taps_ref, 0, start, spread[...])
    halo = halo_ref[...].astype(F32)
    previous = jnp.concatenate([jnp.zeros((LANES - EDGE, STEP), F32), halo], 0).T.astype(BF16)
    for q in range(q_ref.shape[2] // LANES):
        current = q_ref[0, :, q * LANES : (q + 1) * LANES]
        o_ref[:, q * LANES : (q + 1) * LANES] = shaped_tile(previous, current, qtaps[...], shift[...])
        previous = current


def query_call(features, taps, halo):
    _, channels, size = features.shape
    return pl.pallas_call(
        query_kernel,
        grid=(channels // STEP,),
        in_specs=[
            pl.BlockSpec(taps.shape, lambda g: (0, 0, 0)),
            pl.BlockSpec((EDGE, STEP), lambda g: (0, g)),
            pl.BlockSpec((1, STEP, size), lambda g: (0, g, 0)),
        ],
        out_specs=pl.BlockSpec((STEP, size), lambda g: (g, 0)),
        out_shape=pltpu.VMEM((channels, size), F32),
        scratch_shapes=short_scratch(1),
        cost_estimate=pl.CostEstimate(flops=30 * channels * size, bytes_accessed=6 * channels * size, transcendentals=0),
        name="query",
    )(taps, halo, features)


ANY = pl.BlockSpec(memory_space=pl.ANY)


def pair_of(grid_ref, c, own):
    return jnp.concatenate([grid_ref[pl.ds(2 * c + a, N1, stride=own), :] for a in range(2)], 1)


def filter_kernel(half_ref, first_ref, skip_ref, f_ref, table_any, twist_ref, o_any, grid_ref, table, o_ref, sem, o_sem):
    copy = pltpu.make_async_copy(table_any.at[FORWARD, :], table, sem)
    copy.start()
    own = f_ref.shape[0]
    for j in range(N1):
        grid_ref[j * own : (j + 1) * own, :] = f_ref[:, j * N2 : (j + 1) * N2]
    copy.wait()
    twr, twi = twist_ref[:N1], twist_ref[N1:]
    turned = []
    for c in range(own // 2):
        hi, lo = split(pair_of(grid_ref, c, own))
        top, low = table[: 2 * N1], table[2 * N1 : 4 * N1]
        part = mm(top, hi) + mm(low, hi) + mm(top, lo)
        for a in range(2):
            re, im = part[:N1, a * N2 : (a + 1) * N2], part[N1:, a * N2 : (a + 1) * N2]
            turned.append(jnp.concatenate([re * twr - im * twi, re * twi + im * twr], 1))
    copies = []
    for c in range(own):
        spec = mm3(turned[c], table[COLS_HI], table[COLS_LO])
        skip = skip_ref[first_ref[0] + c]
        o_ref[c, :, :N2] = (spec[:, :N2] + skip) * (1.0 / TOTAL)
        o_ref[c, :, N2:] = spec[:, N2:] * (-1.0 / TOTAL)
        if c % 4 == 3:
            done = pl.ds(c - 3, 4)
            copies.append(pltpu.make_async_copy(o_ref.at[done], o_any.at[done], o_sem.at[c // 4]))
            copies[-1].start()
    for copy in copies:
        copy.wait()


def filter_call(filters, skip, half_place, first_channel, own, table, twist):
    return pl.pallas_call(
        filter_kernel,
        grid_spec=pltpu.PrefetchScalarGridSpec(
            num_scalar_prefetch=2,
            grid=(1,),
            in_specs=[
                pl.BlockSpec(memory_space=pltpu.SMEM),
                pl.BlockSpec((own, filters.shape[1]), lambda g, half, first: (half[0], 0)),
                ANY,
                pl.BlockSpec(twist.shape, lambda g, half, first: (0, 0)),
            ],
            out_specs=ANY,
            scratch_shapes=[
                pltpu.VMEM((N1 * own, N2), F32),
                pltpu.VMEM((BACK, N1), BF16),
                pltpu.VMEM((own, N1, 2 * N2), F32),
                pltpu.SemaphoreType.DMA,
                pltpu.SemaphoreType.DMA((own // 4,)),
            ],
        ),
        out_shape=jax.ShapeDtypeStruct((own, N1, 2 * N2), F32),
        compiler_params=pltpu.CompilerParams(vmem_limit_bytes=VMEM_LIMIT),
        cost_estimate=pl.CostEstimate(flops=12 * own * N1 * N1 * 2 * N2, bytes_accessed=6 << 20, transcendentals=0),
        name="filter_spectrum",
    )(half_place.reshape(1), first_channel.reshape(1), skip, filters, table, twist)


PIECES = 4


def conv_kernel(
    own_ref, other_ref, h_any, taps_ref, table, twist, o_any,
    grid_ref, edge_ref, res_ref, h_ref, o_ref, h_sem, o_sem,
):
    own = h_ref.shape[0]
    rows, size = o_ref.shape
    blocks = rows // own
    tiles = size // LANES
    half = blocks // 2
    share = rows // PIECES
    per_piece = half // PIECES
    h_copy = pltpu.make_async_copy(h_any, h_ref, h_sem)
    h_copy.start()

    place = lax.axis_index("half")
    each = block_rows(tiles)
    for ref, side in ((own_ref, place), (other_ref, 1 - place)):
        for i in range(half):
            to = i + side * half
            for q in range(tiles):
                tile = ref[i * each + q * PAIR : i * each + (q + 1) * PAIR, :].astype(F32)
                grid_ref[rows_at(to * tiles + q, own), :] = jnp.where(place == 0, tile[:own], tile[own:])
            edge = ref[i * each + tiles * PAIR : (i + 1) * each, :].astype(F32)
            edge_ref[rows_at(to + 1, own), :] = jnp.where(place == 0, edge, pltpu.roll(edge, LANES // 2, 1))

    edge_ref[:own, :] = jnp.zeros((own, LANES), F32)
    lane = lax.broadcasted_iota(jnp.int32, (rows, LANES), 1)
    both = jnp.where(lane % (LANES // 4) < EDGE, edge_ref[:rows, :], edge_ref[own:, :]).astype(BF16)
    terms = mm(both, table[GATHER : GATHER + LANES, :LANES]).reshape(blocks, own, LANES) * taps_ref[...][None]
    hi, lo = split(terms.reshape(rows, LANES))
    add = table[GATHER + LANES : GATHER + 2 * LANES]
    sums = mm(hi, add) + mm(lo, add)
    gated = sums[:, :LANES] * sums[:, LANES:]
    for p in range(blocks):
        grid_ref[p * tiles * own : (p * tiles + 1) * own, :EDGE] = gated[p * own : (p + 1) * own, :EDGE]

    pairs = range(own // 2)
    twr, twi = twist[:N1], twist[N1:]
    turned = []
    for c in pairs:
        x = pair_of(grid_ref, c, own).astype(BF16)
        part = mm(table[: 2 * N1], x) + mm(table[2 * N1 : 4 * N1], x)
        for a in range(2):
            re, im = part[:N1, a * N2 : (a + 1) * N2], part[N1:, a * N2 : (a + 1) * N2]
            turned.append(jnp.concatenate([re * twr - im * twi, re * twi + im * twr], 1))
    h_copy.wait()
    back = []
    for c in range(own):
        spec = mm3(turned[c], table[COLS_HI], table[COLS_LO])
        sr, si = spec[:, :N2], spec[:, N2:]
        hr, hi = h_ref[c, :, :N2], h_ref[c, :, N2:]
        mid = mm3(jnp.concatenate([sr * hr + si * hi, sr * hi - si * hr], 1), table[COLS_HI], table[COLS_LO])
        mr, mi = mid[:, :N2], mid[:, N2:]
        back.append((mr * twr - mi * twi, mi * twr + mr * twi))
    for c in pairs:
        y = None
        for part in range(2):
            at = BACK + part * N1
            hi, lo = split(jnp.concatenate([back[2 * c][part], back[2 * c + 1][part]], 1))
            top, low = table[at : at + N1], table[at + 2 * N1 : at + 3 * N1]
            term = mm(top, hi) + mm(top, lo) + mm(low, hi)
            y = term if y is None else y + term
        for a in range(2):
            res_ref[pl.ds(2 * c + a, N1, stride=own), :] = y[:, a * N2 : (a + 1) * N2]

    o_copies = []
    for i in range(PIECES):
        for g in range(i * per_piece, (i + 1) * per_piece):
            for q in range(tiles):
                at = [((g + h * half) * tiles + q) * own for h in range(2)]
                tile = jnp.concatenate([res_ref[a : a + own, :] for a in at], 0)
                o_ref[g * 2 * own : (g + 1) * 2 * own, q * LANES : (q + 1) * LANES] = tile.astype(BF16)
        piece = pl.ds(i * share, share)
        o_copies.append(pltpu.make_async_copy(o_ref.at[piece, :], o_any.at[piece, :], o_sem.at[i]))
        o_copies[-1].start()
    for copy in o_copies:
        copy.wait()


def conv_call(blocks, others, spectrum, taps, table, twist, out):
    own = spectrum.shape[0]
    rows = out[0]
    vmem = pl.BlockSpec(memory_space=pltpu.VMEM)
    return pl.pallas_call(
        conv_kernel,
        in_specs=[vmem, vmem, ANY, vmem, vmem, vmem],
        out_specs=ANY,
        out_shape=jax.ShapeDtypeStruct(out, BF16),
        scratch_shapes=[
            pltpu.VMEM((N1 * own, N2), F32),
            pltpu.VMEM((rows + own, LANES), F32),
            pltpu.VMEM((N1 * own, N2), F32),
            pltpu.VMEM(spectrum.shape, F32),
            pltpu.VMEM(out, BF16),
            pltpu.SemaphoreType.DMA,
            pltpu.SemaphoreType.DMA((PIECES,)),
        ],
        compiler_params=pltpu.CompilerParams(vmem_limit_bytes=CONV_LIMIT),
        cost_estimate=pl.CostEstimate(flops=22 * own * N1 * N1 * 2 * N2, bytes_accessed=6 << 20, transcendentals=0),
        name="long_convolution",
    )(blocks, others, spectrum, taps, table, twist)


def shards(features, short_taps, filters, skip):
    size = features.shape[2]
    positions = lax.axis_size("half") * lax.axis_size("ctx")
    own = filters.shape[0] // lax.axis_size("half")
    half_place, ctx_place = lax.axis_index("half"), lax.axis_index("ctx")
    first_channel = ctx_place * filters.shape[0] + half_place * own
    table, twist = transform_tables()
    taps = jnp.swapaxes(short_taps, 0, 1)

    gated = gate_call(features, taps)
    blocks = lax.all_to_all(gated, "ctx", 0, 0, tiled=True)

    tail = features[0, :, size - EDGE :].T
    halo = lax.ppermute(tail, ("half", "ctx"), [(i, i + 1) for i in range(positions - 1)])
    spectrum = filter_call(filters, skip, half_place, first_channel, own, table, twist)
    own_taps = lax.dynamic_slice_in_dim(taps[1:], first_channel, own, 2)
    own_taps = jnp.pad(own_taps.transpose(2, 0, 1), ((0, 0), (0, 0), (0, 8 - TAPS)))
    own_taps = jnp.repeat(own_taps.reshape(own, 16), 8, axis=1)
    blocks, halo, spectrum, own_taps = lax.optimization_barrier((blocks, halo, spectrum, own_taps))
    others = lax.ppermute(blocks, "half", [(0, 1), (1, 0)])

    out = (positions * own, size)
    convolved = conv_call(blocks, others, spectrum, own_taps, table, twist, out)
    back = lax.all_to_all(convolved, ("ctx", "half"), 0, 0, tiled=True)
    query = query_call(features, taps, halo)
    return (query * back.astype(F32)).astype(BF16)


def solution(mesh):
    in_specs = (P("seq", None, ("half", "ctx")), P(), P("ctx", None), P())
    out_specs = P("seq", ("half", "ctx"))
    return jax.shard_map(shards, mesh=mesh, in_specs=in_specs, out_specs=out_specs, check_vma=False)
```

```python
import math

import jax
import jax.numpy as jnp
import ml_dtypes
import numpy as np
from jax import lax
from jax.experimental import pallas as pl
from jax.experimental.pallas import tpu as pltpu
from jax.sharding import PartitionSpec as P

TAPS = 7
EDGE = TAPS - 1
LANES = 128
N1 = 256
N2 = 128
TOTAL = N1 * N2
F32 = jnp.float32
BF16 = jnp.bfloat16


def halves(table):
    hi = table.astype(ml_dtypes.bfloat16)
    lo = (table - hi.astype(np.float64)).astype(ml_dtypes.bfloat16)
    return hi, lo


def transform_tables():
    k1 = np.arange(N1) + 0.25
    first = np.exp(-2j * np.pi * np.outer(k1, np.arange(N1)) / N1)
    twist = np.exp(-2j * np.pi * np.outer(k1, np.arange(N2)) / TOTAL)
    second = np.exp(-2j * np.pi * np.outer(np.arange(N2), np.arange(N2)) / N2)
    rows = np.concatenate([first.real, first.imag], 0)
    columns = np.block([[second.real, second.imag], [-second.imag, second.real]])
    back = np.concatenate([first.real.T, -first.imag.T], 0)
    gather, add = np.zeros((LANES, 2 * LANES)), np.zeros((LANES, 2 * LANES))
    for branch in range(2):
        for j in range(TAPS):
            for t in range(EDGE):
                at = branch * LANES // 2 + j * 8 + t
                gather[branch * LANES // 4 + EDGE + t - j, at] = 1
                add[at, branch * LANES + t] = 1
    exact = [gather.astype(ml_dtypes.bfloat16), add.astype(ml_dtypes.bfloat16)]
    table = np.concatenate([*halves(rows), *halves(columns), *halves(back), *exact], 0)
    return jnp.asarray(table), jnp.asarray(np.concatenate([twist.real, twist.imag], 0).astype(np.float32))


ROWS = slice(0, 4 * N1)
COLS_HI, COLS_LO = slice(4 * N1, 5 * N1), slice(5 * N1, 6 * N1)
BACK = 6 * N1
GATHER = 10 * N1
FORWARD = slice(0, BACK)
VMEM_LIMIT = 60 * 1024 * 1024
CONV_LIMIT = 52428800


def mm(a, b):
    return jnp.dot(a, b, preferred_element_type=F32)


def split(x):
    hi = x.astype(BF16)
    return hi, (x - hi.astype(F32)).astype(BF16)


def mm3(x, whi, wlo):
    hi, lo = split(x)
    return mm(hi, whi) + mm(lo, whi) + mm(hi, wlo)


def rows_at(i, count):
    return pl.ds(pl.multiple_of(i * count, count), count)


GROUP = 8
PAIR = 2 * GROUP


def block_rows(tiles):
    return tiles * PAIR + GROUP


STEP = 256


def fill_selectors(shift_ref, spread_ref):
    shape = shift_ref.shape
    row, col = lax.broadcasted_iota(jnp.int32, shape, 0), lax.broadcasted_iota(jnp.int32, shape, 1)
    shift_ref[...] = jnp.where(row == LANES + col % LANES - (col // LANES + 1), 1.0, 0.0).astype(BF16)
    shape = spread_ref.shape
    row, col = lax.broadcasted_iota(jnp.int32, shape, 0), lax.broadcasted_iota(jnp.int32, shape, 1)
    spread_ref[...] = jnp.where((row < 24) & (row % 8 == col // LANES), 1.0, 0.0).astype(BF16)


def spread_taps(taps_ref, branch, start, spread):
    taps = jnp.concatenate([taps_ref[branch, :, pl.ds(start, STEP)], jnp.zeros((1, STEP), F32)], 0)
    hi = taps.astype(BF16).astype(F32)
    mid = (taps - hi).astype(BF16).astype(F32)
    columns = jnp.concatenate([hi, mid, taps - hi - mid, jnp.zeros((LANES - 24, STEP), F32)], 0).T
    return mm(columns.astype(BF16), spread)


BY_MATRIX = 4


def shaped_tile(previous, current, taps, shift):
    moved = mm(jnp.concatenate([previous, current], 1), shift[:, : BY_MATRIX * LANES])
    before, here = previous.astype(F32), current.astype(F32)
    lane = lax.broadcasted_iota(jnp.int32, here.shape, 1)
    total = taps[:, :LANES] * here
    for j in range(1, TAPS):
        if j <= BY_MATRIX:
            x = moved[:, (j - 1) * LANES : j * LANES]
        else:
            x = pltpu.roll(jnp.where(lane >= LANES - j, before, here), j, 1)
        total = total + taps[:, j * LANES : (j + 1) * LANES] * x
    return total


def gate_kernel(taps_ref, k_ref, v_ref, o_ref, shift, spread, ktaps, vtaps):
    @pl.when(pl.program_id(0) == 0)
    def _():
        fill_selectors(shift, spread)

    start = pl.multiple_of(pl.program_id(0) * STEP, STEP)
    size = k_ref.shape[2]
    tiles = size // LANES
    ktaps[...] = spread_taps(taps_ref, 1, start, spread[...])
    vtaps[...] = spread_taps(taps_ref, 2, start, spread[...])

    def tile(ref, q):
        return ref[0, :, q * LANES : (q + 1) * LANES]

    each = block_rows(tiles)
    blocks = STEP // PAIR
    for q in range(tiles):
        key = shaped_tile(tile(k_ref, (q - 1) % tiles), tile(k_ref, q), ktaps[...], shift[...])
        value = shaped_tile(tile(v_ref, (q - 1) % tiles), tile(v_ref, q), vtaps[...], shift[...])
        gated = (key * value).astype(BF16)
        for d in range(blocks):
            o_ref[d * each + q * PAIR : d * each + (q + 1) * PAIR, :] = gated[d * PAIR : (d + 1) * PAIR]
    lane = lax.broadcasted_iota(jnp.int32, (STEP, LANES), 1)

    def edges(ref, by):
        ends = jnp.where(lane >= LANES - EDGE, tile(ref, tiles - 1).astype(F32), tile(ref, 0).astype(F32))
        return pltpu.roll(ends, by, 1)

    both = jnp.where(lane < LANES // 4, edges(k_ref, EDGE), edges(v_ref, EDGE + LANES // 4))
    moved = pltpu.roll(both, LANES // 2, 1)
    lane = lax.broadcasted_iota(jnp.int32, (GROUP, LANES), 1)
    for d in range(blocks):
        at = d * PAIR
        first, second = both[at : at + GROUP], moved[at + GROUP : at + PAIR]
        o_ref[d * each + tiles * PAIR : (d + 1) * each, :] = jnp.where(lane < LANES // 2, first, second).astype(BF16)


def short_scratch(count):
    return [
        pltpu.VMEM((2 * LANES, BY_MATRIX * LANES), BF16),
        pltpu.VMEM((LANES, TAPS * LANES), BF16),
        *[pltpu.VMEM((STEP, TAPS * LANES), F32)] * count,
    ]


def gate_call(features, taps):
    _, channels, size = features.shape
    each = block_rows(size // LANES)
    return pl.pallas_call(
        gate_kernel,
        grid=(channels // STEP,),
        in_specs=[
            pl.BlockSpec(taps.shape, lambda g: (0, 0, 0)),
            pl.BlockSpec((1, STEP, size), lambda g: (1, g, 0)),
            pl.BlockSpec((1, STEP, size), lambda g: (2, g, 0)),
        ],
        out_specs=pl.BlockSpec((STEP // PAIR * each, LANES), lambda g: (g, 0)),
        out_shape=jax.ShapeDtypeStruct((channels // PAIR * each, LANES), BF16),
        scratch_shapes=short_scratch(2),
        compiler_params=pltpu.CompilerParams(vmem_limit_bytes=VMEM_LIMIT),
        cost_estimate=pl.CostEstimate(flops=60 * channels * size, bytes_accessed=6 * channels * size, transcendentals=0),
        name="gate",
    )(taps, features, features)


def query_kernel(taps_ref, halo_ref, q_ref, o_ref, shift, spread, qtaps):
    @pl.when(pl.program_id(0) == 0)
    def _():
        fill_selectors(shift, spread)

    start = pl.multiple_of(pl.program_id(0) * STEP, STEP)
    qtaps[...] = spread_taps(taps_ref, 0, start, spread[...])
    halo = halo_ref[...].astype(F32)
    previous = jnp.concatenate([jnp.zeros((LANES - EDGE, STEP), F32), halo], 0).T.astype(BF16)
    for q in range(q_ref.shape[2] // LANES):
        current = q_ref[0, :, q * LANES : (q + 1) * LANES]
        o_ref[:, q * LANES : (q + 1) * LANES] = shaped_tile(previous, current, qtaps[...], shift[...])
        previous = current


def query_call(features, taps, halo):
    _, channels, size = features.shape
    return pl.pallas_call(
        query_kernel,
        grid=(channels // STEP,),
        in_specs=[
            pl.BlockSpec(taps.shape, lambda g: (0, 0, 0)),
            pl.BlockSpec((EDGE, STEP), lambda g: (0, g)),
            pl.BlockSpec((1, STEP, size), lambda g: (0, g, 0)),
        ],
        out_specs=pl.BlockSpec((STEP, size), lambda g: (g, 0)),
        out_shape=pltpu.VMEM((channels, size), F32),
        scratch_shapes=short_scratch(1),
        cost_estimate=pl.CostEstimate(flops=30 * channels * size, bytes_accessed=6 * channels * size, transcendentals=0),
        name="query",
    )(taps, halo, features)


ANY = pl.BlockSpec(memory_space=pl.ANY)


def pair_of(grid_ref, c, own):
    return jnp.concatenate([grid_ref[pl.ds(2 * c + a, N1, stride=own), :] for a in range(2)], 1)


def filter_kernel(half_ref, first_ref, skip_ref, f_ref, table_any, twist_ref, o_any, grid_ref, table, o_ref, sem, o_sem):
    copy = pltpu.make_async_copy(table_any.at[FORWARD, :], table, sem)
    copy.start()
    own = f_ref.shape[0]
    for j in range(N1):
        grid_ref[j * own : (j + 1) * own, :] = f_ref[:, j * N2 : (j + 1) * N2]
    copy.wait()
    twr, twi = twist_ref[:N1], twist_ref[N1:]
    turned = []
    for c in range(own // 2):
        hi, lo = split(pair_of(grid_ref, c, own))
        top, low = table[: 2 * N1], table[2 * N1 : 4 * N1]
        part = mm(top, hi) + mm(low, hi) + mm(top, lo)
        for a in range(2):
            re, im = part[:N1, a * N2 : (a + 1) * N2], part[N1:, a * N2 : (a + 1) * N2]
            turned.append(jnp.concatenate([re * twr - im * twi, re * twi + im * twr], 1))
    copies = []
    for c in range(own):
        spec = mm3(turned[c], table[COLS_HI], table[COLS_LO])
        skip = skip_ref[first_ref[0] + c]
        o_ref[c, :, :N2] = (spec[:, :N2] + skip) * (1.0 / TOTAL)
        o_ref[c, :, N2:] = spec[:, N2:] * (-1.0 / TOTAL)
        if c % 4 == 3:
            done = pl.ds(c - 3, 4)
            copies.append(pltpu.make_async_copy(o_ref.at[done], o_any.at[done], o_sem.at[c // 4]))
            copies[-1].start()
    for copy in copies:
        copy.wait()


def filter_call(filters, skip, half_place, first_channel, own, table, twist):
    return pl.pallas_call(
        filter_kernel,
        grid_spec=pltpu.PrefetchScalarGridSpec(
            num_scalar_prefetch=2,
            grid=(1,),
            in_specs=[
                pl.BlockSpec(memory_space=pltpu.SMEM),
                pl.BlockSpec((own, filters.shape[1]), lambda g, half, first: (half[0], 0)),
                ANY,
                pl.BlockSpec(twist.shape, lambda g, half, first: (0, 0)),
            ],
            out_specs=ANY,
            scratch_shapes=[
                pltpu.VMEM((N1 * own, N2), F32),
                pltpu.VMEM((BACK, N1), BF16),
                pltpu.VMEM((own, N1, 2 * N2), F32),
                pltpu.SemaphoreType.DMA,
                pltpu.SemaphoreType.DMA((own // 4,)),
            ],
        ),
        out_shape=jax.ShapeDtypeStruct((own, N1, 2 * N2), F32),
        compiler_params=pltpu.CompilerParams(vmem_limit_bytes=VMEM_LIMIT),
        cost_estimate=pl.CostEstimate(flops=12 * own * N1 * N1 * 2 * N2, bytes_accessed=6 << 20, transcendentals=0),
        name="filter_spectrum",
    )(half_place.reshape(1), first_channel.reshape(1), skip, filters, table, twist)


PIECES = 2


def conv_kernel(
    own_ref, other_ref, h_any, taps_ref, table, twist, o_any,
    grid_ref, edge_ref, res_ref, h_ref, o_ref, h_sem, o_sem,
):
    own = h_ref.shape[0]
    rows, size = o_ref.shape
    blocks = rows // own
    tiles = size // LANES
    half = blocks // 2
    share = rows // PIECES
    per_piece = half // PIECES
    h_copy = pltpu.make_async_copy(h_any, h_ref, h_sem)
    h_copy.start()

    place = lax.axis_index("half")
    each = block_rows(tiles)
    for ref, side in ((own_ref, place), (other_ref, 1 - place)):
        for i in range(half):
            to = i + side * half
            for q in range(tiles):
                tile = ref[i * each + q * PAIR : i * each + (q + 1) * PAIR, :].astype(F32)
                grid_ref[rows_at(to * tiles + q, own), :] = jnp.where(place == 0, tile[:own], tile[own:])
            edge = ref[i * each + tiles * PAIR : (i + 1) * each, :].astype(F32)
            edge_ref[rows_at(to + 1, own), :] = jnp.where(place == 0, edge, pltpu.roll(edge, LANES // 2, 1))

    edge_ref[:own, :] = jnp.zeros((own, LANES), F32)
    lane = lax.broadcasted_iota(jnp.int32, (rows, LANES), 1)
    both = jnp.where(lane % (LANES // 4) < EDGE, edge_ref[:rows, :], edge_ref[own:, :]).astype(BF16)
    terms = mm(both, table[GATHER : GATHER + LANES, :LANES]).reshape(blocks, own, LANES) * taps_ref[...][None]
    hi, lo = split(terms.reshape(rows, LANES))
    add = table[GATHER + LANES : GATHER + 2 * LANES]
    sums = mm(hi, add) + mm(lo, add)
    gated = sums[:, :LANES] * sums[:, LANES:]
    for p in range(blocks):
        grid_ref[p * tiles * own : (p * tiles + 1) * own, :EDGE] = gated[p * own : (p + 1) * own, :EDGE]

    pairs = range(own // 2)
    twr, twi = twist[:N1], twist[N1:]
    turned = []
    for c in pairs:
        x = pair_of(grid_ref, c, own).astype(BF16)
        part = mm(table[: 2 * N1], x) + mm(table[2 * N1 : 4 * N1], x)
        for a in range(2):
            re, im = part[:N1, a * N2 : (a + 1) * N2], part[N1:, a * N2 : (a + 1) * N2]
            turned.append(jnp.concatenate([re * twr - im * twi, re * twi + im * twr], 1))
    h_copy.wait()
    back = []
    for c in range(own):
        spec = mm3(turned[c], table[COLS_HI], table[COLS_LO])
        sr, si = spec[:, :N2], spec[:, N2:]
        hr, hi = h_ref[c, :, :N2], h_ref[c, :, N2:]
        mid = mm3(jnp.concatenate([sr * hr + si * hi, sr * hi - si * hr], 1), table[COLS_HI], table[COLS_LO])
        mr, mi = mid[:, :N2], mid[:, N2:]
        back.append((mr * twr - mi * twi, mi * twr + mr * twi))
    parts = []
    for c in pairs:
        for part in range(2):
            parts.append(split(jnp.concatenate([back[2 * c][part], back[2 * c + 1][part]], 1)))
    o_copies = []
    stretch = N1 // 2 // PIECES
    for i in range(PIECES):
        cuts = [h * (N1 // 2) + i * stretch for h in range(2)]
        for c in pairs:
            y = None
            for part in range(2):
                top, low = (
                    jnp.concatenate([table[at + cut : at + cut + stretch] for cut in cuts], 0)
                    for at in (BACK + part * N1, BACK + (part + 2) * N1)
                )
                hi, lo = parts[2 * c + part]
                term = mm(top, hi) + mm(top, lo) + mm(low, hi)
                y = term if y is None else y + term
            for a in range(2):
                for h, cut in enumerate(cuts):
                    piece = y[h * stretch : (h + 1) * stretch, a * N2 : (a + 1) * N2]
                    res_ref[pl.ds(cut * own + 2 * c + a, stretch, stride=own), :] = piece
        for g in range(i * per_piece, (i + 1) * per_piece):
            for q in range(tiles):
                at = [((g + h * half) * tiles + q) * own for h in range(2)]
                tile = jnp.concatenate([res_ref[a : a + own, :] for a in at], 0)
                o_ref[g * 2 * own : (g + 1) * 2 * own, q * LANES : (q + 1) * LANES] = tile.astype(BF16)
        piece = pl.ds(i * share, share)
        o_copies.append(pltpu.make_async_copy(o_ref.at[piece, :], o_any.at[piece, :], o_sem.at[i]))
        o_copies[-1].start()
    for copy in o_copies:
        copy.wait()


def conv_call(blocks, others, spectrum, taps, table, twist, out):
    own = spectrum.shape[0]
    rows = out[0]
    vmem = pl.BlockSpec(memory_space=pltpu.VMEM)
    return pl.pallas_call(
        conv_kernel,
        in_specs=[vmem, vmem, ANY, vmem, vmem, vmem],
        out_specs=ANY,
        out_shape=jax.ShapeDtypeStruct(out, BF16),
        scratch_shapes=[
            pltpu.VMEM((N1 * own, N2), F32),
            pltpu.VMEM((rows + own, LANES), F32),
            pltpu.VMEM((N1 * own, N2), F32),
            pltpu.VMEM(spectrum.shape, F32),
            pltpu.VMEM(out, BF16),
            pltpu.SemaphoreType.DMA,
            pltpu.SemaphoreType.DMA((PIECES,)),
        ],
        compiler_params=pltpu.CompilerParams(vmem_limit_bytes=CONV_LIMIT),
        cost_estimate=pl.CostEstimate(flops=22 * own * N1 * N1 * 2 * N2, bytes_accessed=6 << 20, transcendentals=0),
        name="long_convolution",
    )(blocks, others, spectrum, taps, table, twist)


def shards(features, short_taps, filters, skip):
    size = features.shape[2]
    positions = lax.axis_size("half") * lax.axis_size("ctx")
    own = filters.shape[0] // lax.axis_size("half")
    half_place, ctx_place = lax.axis_index("half"), lax.axis_index("ctx")
    first_channel = ctx_place * filters.shape[0] + half_place * own
    table, twist = transform_tables()
    taps = jnp.swapaxes(short_taps, 0, 1)

    gated = gate_call(features, taps)
    blocks = lax.all_to_all(gated, "ctx", 0, 0, tiled=True)

    tail = features[0, :, size - EDGE :].T
    halo = lax.ppermute(tail, ("half", "ctx"), [(i, i + 1) for i in range(positions - 1)])
    spectrum = filter_call(filters, skip, half_place, first_channel, own, table, twist)
    own_taps = lax.dynamic_slice_in_dim(taps[1:], first_channel, own, 2)
    own_taps = jnp.pad(own_taps.transpose(2, 0, 1), ((0, 0), (0, 0), (0, 8 - TAPS)))
    own_taps = jnp.repeat(own_taps.reshape(own, 16), 8, axis=1)
    blocks, halo, spectrum, own_taps = lax.optimization_barrier((blocks, halo, spectrum, own_taps))
    others = lax.ppermute(blocks, "half", [(0, 1), (1, 0)])

    out = (positions * own, size)
    convolved = conv_call(blocks, others, spectrum, own_taps, table, twist, out)
    back = lax.all_to_all(convolved, ("ctx", "half"), 0, 0, tiled=True)
    query = query_call(features, taps, halo)
    return (query * back.astype(F32)).astype(BF16)


def solution(mesh):
    in_specs = (P("seq", None, ("half", "ctx")), P(), P("ctx", None), P())
    out_specs = P("seq", ("half", "ctx"))
    return jax.shard_map(shards, mesh=mesh, in_specs=in_specs, out_specs=out_specs, check_vma=False)
```

```python
import math

import jax
import jax.numpy as jnp
import ml_dtypes
import numpy as np
from jax import lax
from jax.experimental import pallas as pl
from jax.experimental.pallas import tpu as pltpu
from jax.sharding import PartitionSpec as P

TAPS = 7
EDGE = TAPS - 1
LANES = 128
N1 = 256
N2 = 128
TOTAL = N1 * N2
F32 = jnp.float32
BF16 = jnp.bfloat16


def halves(table):
    hi = table.astype(ml_dtypes.bfloat16)
    lo = (table - hi.astype(np.float64)).astype(ml_dtypes.bfloat16)
    return hi, lo


def transform_tables():
    k1 = np.arange(N1) + 0.25
    first = np.exp(-2j * np.pi * np.outer(k1, np.arange(N1)) / N1)
    twist = np.exp(-2j * np.pi * np.outer(k1, np.arange(N2)) / TOTAL)
    second = np.exp(-2j * np.pi * np.outer(np.arange(N2), np.arange(N2)) / N2)
    rows = np.concatenate([first.real, first.imag], 0)
    columns = np.block([[second.real, second.imag], [-second.imag, second.real]])
    back = np.concatenate([first.real.T, -first.imag.T], 0)
    gather, add = np.zeros((LANES, 2 * LANES)), np.zeros((LANES, 2 * LANES))
    for branch in range(2):
        for j in range(TAPS):
            for t in range(EDGE):
                at = branch * LANES // 2 + j * 8 + t
                gather[branch * LANES // 4 + EDGE + t - j, at] = 1
                add[at, branch * LANES + t] = 1
    exact = [gather.astype(ml_dtypes.bfloat16), add.astype(ml_dtypes.bfloat16)]
    table = np.concatenate([*halves(rows), *halves(columns), *halves(back), *exact], 0)
    return jnp.asarray(table), jnp.asarray(np.concatenate([twist.real, twist.imag], 0).astype(np.float32))


ROWS = slice(0, 4 * N1)
COLS_HI, COLS_LO = slice(4 * N1, 5 * N1), slice(5 * N1, 6 * N1)
BACK = 6 * N1
GATHER = 10 * N1
FORWARD = slice(0, BACK)
VMEM_LIMIT = 60 * 1024 * 1024
CONV_LIMIT = 52428800


def mm(a, b):
    return jnp.dot(a, b, preferred_element_type=F32)


def split(x):
    hi = x.astype(BF16)
    return hi, (x - hi.astype(F32)).astype(BF16)


def mm3(x, whi, wlo):
    hi, lo = split(x)
    return mm(hi, whi) + mm(lo, whi) + mm(hi, wlo)


def rows_at(i, count):
    return pl.ds(pl.multiple_of(i * count, count), count)


GROUP = 8
PAIR = 2 * GROUP


def block_rows(tiles):
    return tiles * PAIR + GROUP


STEP = 256


def fill_selectors(shift_ref, spread_ref):
    shape = shift_ref.shape
    row, col = lax.broadcasted_iota(jnp.int32, shape, 0), lax.broadcasted_iota(jnp.int32, shape, 1)
    shift_ref[...] = jnp.where(row == LANES + col % LANES - (col // LANES + 1), 1.0, 0.0).astype(BF16)
    shape = spread_ref.shape
    row, col = lax.broadcasted_iota(jnp.int32, shape, 0), lax.broadcasted_iota(jnp.int32, shape, 1)
    spread_ref[...] = jnp.where((row < 24) & (row % 8 == col // LANES), 1.0, 0.0).astype(BF16)


def spread_taps(taps_ref, branch, start, spread):
    taps = jnp.concatenate([taps_ref[branch, :, pl.ds(start, STEP)], jnp.zeros((1, STEP), F32)], 0)
    hi = taps.astype(BF16).astype(F32)
    mid = (taps - hi).astype(BF16).astype(F32)
    columns = jnp.concatenate([hi, mid, taps - hi - mid, jnp.zeros((LANES - 24, STEP), F32)], 0).T
    return mm(columns.astype(BF16), spread)


BY_MATRIX = 4


def shaped_tile(previous, current, taps, shift):
    moved = mm(jnp.concatenate([previous, current], 1), shift[:, : BY_MATRIX * LANES])
    before, here = previous.astype(F32), current.astype(F32)
    lane = lax.broadcasted_iota(jnp.int32, here.shape, 1)
    total = taps[:, :LANES] * here
    for j in range(1, TAPS):
        if j <= BY_MATRIX:
            x = moved[:, (j - 1) * LANES : j * LANES]
        else:
            x = pltpu.roll(jnp.where(lane >= LANES - j, before, here), j, 1)
        total = total + taps[:, j * LANES : (j + 1) * LANES] * x
    return total


def gate_kernel(taps_ref, k_ref, v_ref, o_ref, shift, spread, ktaps, vtaps):
    @pl.when(pl.program_id(0) == 0)
    def _():
        fill_selectors(shift, spread)

    start = pl.multiple_of(pl.program_id(0) * STEP, STEP)
    size = k_ref.shape[2]
    tiles = size // LANES
    ktaps[...] = spread_taps(taps_ref, 1, start, spread[...])
    vtaps[...] = spread_taps(taps_ref, 2, start, spread[...])

    def tile(ref, q):
        return ref[0, :, q * LANES : (q + 1) * LANES]

    each = block_rows(tiles)
    blocks = STEP // PAIR
    for q in range(tiles):
        key = shaped_tile(tile(k_ref, (q - 1) % tiles), tile(k_ref, q), ktaps[...], shift[...])
        value = shaped_tile(tile(v_ref, (q - 1) % tiles), tile(v_ref, q), vtaps[...], shift[...])
        gated = (key * value).astype(BF16)
        for d in range(blocks):
            o_ref[d * each + q * PAIR : d * each + (q + 1) * PAIR, :] = gated[d * PAIR : (d + 1) * PAIR]
    lane = lax.broadcasted_iota(jnp.int32, (STEP, LANES), 1)

    def edges(ref, by):
        ends = jnp.where(lane >= LANES - EDGE, tile(ref, tiles - 1).astype(F32), tile(ref, 0).astype(F32))
        return pltpu.roll(ends, by, 1)

    both = jnp.where(lane < LANES // 4, edges(k_ref, EDGE), edges(v_ref, EDGE + LANES // 4))
    moved = pltpu.roll(both, LANES // 2, 1)
    lane = lax.broadcasted_iota(jnp.int32, (GROUP, LANES), 1)
    for d in range(blocks):
        at = d * PAIR
        first, second = both[at : at + GROUP], moved[at + GROUP : at + PAIR]
        o_ref[d * each + tiles * PAIR : (d + 1) * each, :] = jnp.where(lane < LANES // 2, first, second).astype(BF16)


def short_scratch(count):
    return [
        pltpu.VMEM((2 * LANES, BY_MATRIX * LANES), BF16),
        pltpu.VMEM((LANES, TAPS * LANES), BF16),
        *[pltpu.VMEM((STEP, TAPS * LANES), F32)] * count,
    ]


def gate_call(features, taps):
    _, channels, size = features.shape
    each = block_rows(size // LANES)
    return pl.pallas_call(
        gate_kernel,
        grid=(channels // STEP,),
        in_specs=[
            pl.BlockSpec(taps.shape, lambda g: (0, 0, 0)),
            pl.BlockSpec((1, STEP, size), lambda g: (1, g, 0)),
            pl.BlockSpec((1, STEP, size), lambda g: (2, g, 0)),
        ],
        out_specs=pl.BlockSpec((STEP // PAIR * each, LANES), lambda g: (g, 0)),
        out_shape=jax.ShapeDtypeStruct((channels // PAIR * each, LANES), BF16),
        scratch_shapes=short_scratch(2),
        compiler_params=pltpu.CompilerParams(vmem_limit_bytes=VMEM_LIMIT),
        cost_estimate=pl.CostEstimate(flops=60 * channels * size, bytes_accessed=6 * channels * size, transcendentals=0),
        name="gate",
    )(taps, features, features)


def query_kernel(taps_ref, halo_ref, q_ref, o_ref, shift, spread, qtaps):
    @pl.when(pl.program_id(0) == 0)
    def _():
        fill_selectors(shift, spread)

    start = pl.multiple_of(pl.program_id(0) * STEP, STEP)
    qtaps[...] = spread_taps(taps_ref, 0, start, spread[...])
    halo = halo_ref[...].astype(F32)
    previous = jnp.concatenate([jnp.zeros((LANES - EDGE, STEP), F32), halo], 0).T.astype(BF16)
    for q in range(q_ref.shape[2] // LANES):
        current = q_ref[0, :, q * LANES : (q + 1) * LANES]
        o_ref[:, q * LANES : (q + 1) * LANES] = shaped_tile(previous, current, qtaps[...], shift[...])
        previous = current


def query_call(features, taps, halo):
    _, channels, size = features.shape
    return pl.pallas_call(
        query_kernel,
        grid=(channels // STEP,),
        in_specs=[
            pl.BlockSpec(taps.shape, lambda g: (0, 0, 0)),
            pl.BlockSpec((EDGE, STEP), lambda g: (0, g)),
            pl.BlockSpec((1, STEP, size), lambda g: (0, g, 0)),
        ],
        out_specs=pl.BlockSpec((STEP, size), lambda g: (g, 0)),
        out_shape=pltpu.VMEM((channels, size), F32),
        scratch_shapes=short_scratch(1),
        cost_estimate=pl.CostEstimate(flops=30 * channels * size, bytes_accessed=6 * channels * size, transcendentals=0),
        name="query",
    )(taps, halo, features)


ANY = pl.BlockSpec(memory_space=pl.ANY)


def pair_of(grid_ref, c, own):
    return jnp.concatenate([grid_ref[pl.ds(2 * c + a, N1, stride=own), :] for a in range(2)], 1)


def filter_kernel(place_ref, skip_ref, f_ref, table_any, twist_ref, o_ref, grid_ref, table, sem):
    copy = pltpu.make_async_copy(table_any.at[FORWARD, :], table, sem)
    copy.start()
    own = f_ref.shape[0]
    for j in range(N1):
        grid_ref[j * own : (j + 1) * own, :] = f_ref[:, j * N2 : (j + 1) * N2]
    copy.wait()

    def pair(c, carry):
        hi, lo = split(pair_of(grid_ref, c, own))
        top, low = table[: 2 * N1], table[2 * N1 : 4 * N1]
        part = mm(top, hi) + mm(low, hi) + mm(top, lo)
        twr, twi = twist_ref[:N1], twist_ref[N1:]
        for a in range(2):
            re, im = part[:N1, a * N2 : (a + 1) * N2], part[N1:, a * N2 : (a + 1) * N2]
            turned = jnp.concatenate([re * twr - im * twi, re * twi + im * twr], 1)
            spec = mm3(turned, table[COLS_HI], table[COLS_LO])
            skip = skip_ref[place_ref[1] + 2 * c + a]
            o_ref[2 * c + a, :, :N2] = (spec[:, :N2] + skip) * (1.0 / TOTAL)
            o_ref[2 * c + a, :, N2:] = spec[:, N2:] * (-1.0 / TOTAL)
        return carry

    lax.fori_loop(0, own // 2, pair, 0)


def filter_call(filters, skip, half_place, first_channel, own, table, twist):
    return pl.pallas_call(
        filter_kernel,
        grid_spec=pltpu.PrefetchScalarGridSpec(
            num_scalar_prefetch=1,
            grid=(1,),
            in_specs=[
                pl.BlockSpec(memory_space=pltpu.SMEM),
                pl.BlockSpec((own, filters.shape[1]), lambda g, place: (place[0], 0)),
                ANY,
                pl.BlockSpec(twist.shape, lambda g, place: (0, 0)),
            ],
            out_specs=pl.BlockSpec((own, N1, 2 * N2), lambda g, place: (0, 0, 0)),
            scratch_shapes=[pltpu.VMEM((N1 * own, N2), F32), pltpu.VMEM((BACK, N1), BF16), pltpu.SemaphoreType.DMA],
        ),
        out_shape=jax.ShapeDtypeStruct((own, N1, 2 * N2), F32),
        compiler_params=pltpu.CompilerParams(vmem_limit_bytes=VMEM_LIMIT),
        cost_estimate=pl.CostEstimate(flops=12 * own * N1 * N1 * 2 * N2, bytes_accessed=6 << 20, transcendentals=0),
        name="filter_spectrum",
    )(jnp.stack([half_place, first_channel]).astype(jnp.int32), skip, filters, table, twist)


PIECES = 4


def conv_kernel(
    own_ref, other_ref, h_any, taps_ref, table, twist, o_any,
    grid_ref, edge_ref, res_ref, h_ref, o_ref, h_sem, o_sem,
):
    own = h_ref.shape[0]
    rows, size = o_ref.shape
    blocks = rows // own
    tiles = size // LANES
    half = blocks // 2
    share = rows // PIECES
    per_piece = half // PIECES
    h_copy = pltpu.make_async_copy(h_any, h_ref, h_sem)
    h_copy.start()

    place = lax.axis_index("half")
    each = block_rows(tiles)
    for ref, side in ((own_ref, place), (other_ref, 1 - place)):
        for i in range(half):
            to = i + side * half
            for q in range(tiles):
                tile = ref[i * each + q * PAIR : i * each + (q + 1) * PAIR, :].astype(F32)
                grid_ref[rows_at(to * tiles + q, own), :] = jnp.where(place == 0, tile[:own], tile[own:])
            edge = ref[i * each + tiles * PAIR : (i + 1) * each, :].astype(F32)
            edge_ref[rows_at(to + 1, own), :] = jnp.where(place == 0, edge, pltpu.roll(edge, LANES // 2, 1))

    edge_ref[:own, :] = jnp.zeros((own, LANES), F32)
    lane = lax.broadcasted_iota(jnp.int32, (rows, LANES), 1)
    both = jnp.where(lane % (LANES // 4) < EDGE, edge_ref[:rows, :], edge_ref[own:, :]).astype(BF16)
    terms = mm(both, table[GATHER : GATHER + LANES, :LANES]).reshape(blocks, own, LANES) * taps_ref[...][None]
    hi, lo = split(terms.reshape(rows, LANES))
    add = table[GATHER + LANES : GATHER + 2 * LANES]
    sums = mm(hi, add) + mm(lo, add)
    gated = sums[:, :LANES] * sums[:, LANES:]
    for p in range(blocks):
        grid_ref[p * tiles * own : (p * tiles + 1) * own, :EDGE] = gated[p * own : (p + 1) * own, :EDGE]

    pairs = range(own // 2)
    twr, twi = twist[:N1], twist[N1:]
    turned = []
    for c in pairs:
        x = pair_of(grid_ref, c, own).astype(BF16)
        part = mm(table[: 2 * N1], x) + mm(table[2 * N1 : 4 * N1], x)
        for a in range(2):
            re, im = part[:N1, a * N2 : (a + 1) * N2], part[N1:, a * N2 : (a + 1) * N2]
            turned.append(jnp.concatenate([re * twr - im * twi, re * twi + im * twr], 1))
    h_copy.wait()
    back = []
    for c in range(own):
        spec = mm3(turned[c], table[COLS_HI], table[COLS_LO])
        sr, si = spec[:, :N2], spec[:, N2:]
        hr, hi = h_ref[c, :, :N2], h_ref[c, :, N2:]
        mid = mm3(jnp.concatenate([sr * hr + si * hi, sr * hi - si * hr], 1), table[COLS_HI], table[COLS_LO])
        mr, mi = mid[:, :N2], mid[:, N2:]
        back.append((mr * twr - mi * twi, mi * twr + mr * twi))
    for c in pairs:
        y = None
        for part in range(2):
            at = BACK + part * N1
            hi, lo = split(jnp.concatenate([back[2 * c][part], back[2 * c + 1][part]], 1))
            top, low = table[at : at + N1], table[at + 2 * N1 : at + 3 * N1]
            term = mm(top, hi) + mm(top, lo) + mm(low, hi)
            y = term if y is None else y + term
        for a in range(2):
            res_ref[pl.ds(2 * c + a, N1, stride=own), :] = y[:, a * N2 : (a + 1) * N2]

    o_copies = []
    for i in range(PIECES):
        for g in range(i * per_piece, (i + 1) * per_piece):
            for q in range(tiles):
                at = [((g + h * half) * tiles + q) * own for h in range(2)]
                tile = jnp.concatenate([res_ref[a : a + own, :] for a in at], 0)
                o_ref[g * 2 * own : (g + 1) * 2 * own, q * LANES : (q + 1) * LANES] = tile.astype(BF16)
        piece = pl.ds(i * share, share)
        o_copies.append(pltpu.make_async_copy(o_ref.at[piece, :], o_any.at[piece, :], o_sem.at[i]))
        o_copies[-1].start()
    for copy in o_copies:
        copy.wait()


def conv_call(blocks, others, spectrum, taps, table, twist, out):
    own = spectrum.shape[0]
    rows = out[0]
    vmem = pl.BlockSpec(memory_space=pltpu.VMEM)
    return pl.pallas_call(
        conv_kernel,
        in_specs=[vmem, vmem, ANY, vmem, vmem, vmem],
        out_specs=ANY,
        out_shape=jax.ShapeDtypeStruct(out, BF16),
        scratch_shapes=[
            pltpu.VMEM((N1 * own, N2), F32),
            pltpu.VMEM((rows + own, LANES), F32),
            pltpu.VMEM((N1 * own, N2), F32),
            pltpu.VMEM(spectrum.shape, F32),
            pltpu.VMEM(out, BF16),
            pltpu.SemaphoreType.DMA,
            pltpu.SemaphoreType.DMA((PIECES,)),
        ],
        compiler_params=pltpu.CompilerParams(vmem_limit_bytes=CONV_LIMIT),
        cost_estimate=pl.CostEstimate(flops=22 * own * N1 * N1 * 2 * N2, bytes_accessed=6 << 20, transcendentals=0),
        name="long_convolution",
    )(blocks, others, spectrum, taps, table, twist)


def shards(features, short_taps, filters, skip):
    size = features.shape[2]
    positions = lax.axis_size("half") * lax.axis_size("ctx")
    own = filters.shape[0] // lax.axis_size("half")
    half_place, ctx_place = lax.axis_index("half"), lax.axis_index("ctx")
    first_channel = ctx_place * filters.shape[0] + half_place * own
    table, twist = transform_tables()
    taps = jnp.swapaxes(short_taps, 0, 1)

    gated = gate_call(features, taps)
    blocks = lax.all_to_all(gated, "ctx", 0, 0, tiled=True)

    tail = features[0, :, size - EDGE :].T
    halo = lax.ppermute(tail, ("half", "ctx"), [(i, i + 1) for i in range(positions - 1)])
    spectrum = filter_call(filters, skip, half_place, first_channel, own, table, twist)
    own_taps = lax.dynamic_slice_in_dim(taps[1:], first_channel, own, 2)
    own_taps = jnp.pad(own_taps.transpose(2, 0, 1), ((0, 0), (0, 0), (0, 8 - TAPS)))
    own_taps = jnp.repeat(own_taps.reshape(own, 16), 8, axis=1)
    blocks, halo, spectrum, own_taps = lax.optimization_barrier((blocks, halo, spectrum, own_taps))
    others = lax.ppermute(blocks, "half", [(0, 1), (1, 0)])

    out = (positions * own, size)
    convolved = conv_call(blocks, others, spectrum, own_taps, table, twist, out)
    back = lax.all_to_all(convolved, ("ctx", "half"), 0, 0, tiled=True)
    query = query_call(features, taps, halo)
    return (query * back.astype(F32)).astype(BF16)


def solution(mesh):
    in_specs = (P("seq", None, ("half", "ctx")), P(), P("ctx", None), P())
    out_specs = P("seq", ("half", "ctx"))
    return jax.shard_map(shards, mesh=mesh, in_specs=in_specs, out_specs=out_specs, check_vma=False)
```
